32 devices in a mesh: section: 4 (over y, x), fsdp: 8 (over z, core).
Axes of the slice: x: 2, y: 2, z: 4, core: 2. Of those that a mesh axis runs over, the one named last changes fastest.
Arguments:
- section_inputs: bfloat16 [4, 2, 1024, 8192], P('section', None, 'fsdp'), may hold values from -6 to 6
- top_grads: bfloat16 [2, 1024, 8192], P(None, 'fsdp'), may hold values from -6 to 6
- weights: bfloat16 [4, 8192, 512], P('section', 'fsdp'), may hold values from -0.125 to 0.125
- norm_gains: float32 [4, 8192], P('section', 'fsdp'), may hold values from 0.25 to 1.75
- feedback: float32 [4, 1024, 8192], P('section', 'fsdp'), may hold values from -4 to 4
- rotation_bits: int32 [4, 8192], replicated, may hold values from 0 to 1
- batch_order: int32 [2], replicated, may hold values from 0 to 1, each once
Outputs:
- input_grads: float32 [4, 2, 1024, 8192], P('section', None, 'fsdp')
- weight_grads: float32 [4, 8192, 512], P('section', 'fsdp')
- gain_grads: float32 [4, 8192], P('section', 'fsdp')
- feedback_out: float32 [4, 1024, 8192], P('section', 'fsdp')
The draws below stay inside these ranges and needn't reach their ends.
Inputs may be any that keep to these rules, and one draw needn't show every extreme that they name: `batch_order`: a permutation of the micro-batches.
All inputs are finite; a program needn't handle non-finite values.
Results may differ from the reference program's by a relative error of at most 0.035.
Values may be sent and summed in bfloat16 or wider, within the bound.
A program may use at most 192 MiB of HBM per device.

```python
import jax
import jax.numpy as jnp
from jax import lax

D = 8192
R = 512
HB = 256
MB = 2
TOKENS = 1024
N_SECTION = 4


def set_ends(result, stream_key, low, top_value):
    spot = [jax.random.randint(jax.random.fold_in(stream_key, axis), (), 0, length) for axis, length in enumerate(result.shape)]
    longest = result.shape.index(max(result.shape))
    neighbour = spot[:longest] + [(spot[longest] + 1) % result.shape[longest]] + spot[longest + 1:]
    return result.at[tuple(spot)].set(low).at[tuple(neighbour)].set(top_value)


def block_levels(stream_key, dims, shards, smallest, top_value):
    level = 1.0
    for dim, shards_of in shards:
        draws = jax.random.uniform(jax.random.fold_in(jax.random.fold_in(stream_key, 6), dim), (shards_of,), jnp.float32, smallest / len(shards), top_value / len(shards))
        level = level * jnp.repeat(jnp.exp(draws), dims[dim] // shards_of).reshape((-1,) + (1,) * (len(dims) - 1 - dim))
    return level


def normal_values(own_key, shape, scale, reach, shards=(), kind=jnp.bfloat16):
    array = scale * jax.random.normal(own_key, shape, jnp.float32)
    if shards:
        array = array * block_levels(own_key, shape, shards, -0.22, 0.18)
    return jnp.clip(array, -reach, reach).astype(kind)


def setup_inputs(seed: int = 0) -> dict:
    splits = jax.random.split(jax.random.key(seed), 8)
    section_inputs = normal_values(splits[0], (N_SECTION, MB, TOKENS, D), 1.0, 6.0, ((0, 4), (2, 8)))
    top_grads = normal_values(splits[1], (MB, TOKENS, D), 1.0, 6.0, ((1, 8),))
    weights = normal_values(splits[2], (N_SECTION, D, R), (D // 4) ** -0.5, 0.125, ((0, 4), (1, 8)))
    norm_gains = jnp.clip(1.0 + 0.15 * jax.random.normal(splits[3], (N_SECTION, D), jnp.float32), 0.25, 1.75)
    feedback = normal_values(splits[4], (N_SECTION, TOKENS, D), 0.5, 4.0, ((0, 4), (1, 8)), jnp.float32)
    rotation_bits = set_ends(jax.random.randint(splits[5], (N_SECTION, D), 0, 2), jax.random.fold_in(splits[5], 1), 0, 1).astype(jnp.int32)
    batch_order = jax.random.permutation(splits[6], MB).astype(jnp.int32)
    return dict(section_inputs=section_inputs, top_grads=top_grads, weights=weights, norm_gains=norm_gains, feedback=feedback, rotation_bits=rotation_bits, batch_order=batch_order)


eps_norm = 1e-05
eps_scale = 1e-06
highest = lax.Precision.HIGHEST

def hadamard(order_size):
    position = jnp.arange(order_size, dtype=jnp.int32)
    shared_bits = jnp.bitwise_and(position[:, None], position[None, :])
    parity = jnp.zeros((order_size, order_size), jnp.int32)
    for bit_place in range(order_size.bit_length() - 1):
        parity = parity + jnp.bitwise_and(jnp.right_shift(shared_bits, bit_place), 1)
    return (1 - 2 * (parity % 2)).astype(jnp.float32) / jnp.sqrt(jnp.float32(order_size))

def rotate(values, sign_row, matrix):
    block_size = matrix.shape[0]
    blocks = (values * sign_row).reshape(values.shape[0], values.shape[1] // block_size, block_size)
    return jnp.einsum('tbk,kj->tbj', blocks, matrix, precision=highest)

def restore(rotated, sign_row, matrix):
    unrotated = jnp.einsum('tbk,kj->tbj', rotated, matrix, precision=highest)
    return unrotated.reshape(unrotated.shape[0], -1) * sign_row

def layer_backward(inputs, grad_in, gain_row, weight):
    values = inputs.astype(jnp.float32)
    scale_inv = lax.rsqrt(lax.optimization_barrier(jnp.mean(values * values, axis=-1, keepdims=True)) + eps_norm)
    normed = values * scale_inv
    hidden_in = (normed * gain_row).astype(jnp.bfloat16)
    grad_low = grad_in.astype(jnp.bfloat16)
    pre = jnp.dot(hidden_in, weight, preferred_element_type=jnp.float32)
    grad_act = jnp.dot(grad_low, weight, preferred_element_type=jnp.float32)
    sigma = jax.nn.sigmoid(pre)
    active_out = (pre * sigma).astype(jnp.bfloat16)
    grad_pre = (grad_act * sigma * (1.0 + pre * (1.0 - sigma))).astype(jnp.bfloat16)
    grad_hidden = lax.dot_general(grad_pre, weight, (((1,), (1,)), ((), ())), preferred_element_type=jnp.float32)
    gain_term = lax.optimization_barrier(jnp.sum(grad_hidden * normed, axis=0))
    grad_normed = grad_hidden * gain_row
    grad_out = grad_in + scale_inv * (grad_normed - normed * lax.optimization_barrier(jnp.mean(grad_normed * normed, axis=-1, keepdims=True)))
    return (grad_out, gain_term, hidden_in, grad_low, grad_pre, active_out)

def encode(grad_out, carried, sign_row, matrix):
    total = grad_out + carried
    rotated = rotate(total, sign_row, matrix)
    scale_low = (lax.optimization_barrier(jnp.mean(jnp.abs(rotated), axis=-1)) + eps_scale).astype(jnp.bfloat16)
    scale_wide = scale_low.astype(jnp.float32)[..., None]
    levels = jnp.clip(rotated / scale_wide, -1.0, 1.0).astype(jnp.bfloat16)
    decoded = restore(levels.astype(jnp.float32) * scale_wide, sign_row, matrix)
    return (total - decoded, decoded)

def reference(section_inputs, top_grads, weights, norm_gains, feedback, rotation_bits, batch_order):
    matrix = hadamard(HB)
    sign_rows = (1 - 2 * rotation_bits).astype(jnp.float32)
    adapter = weights.shape[2]
    carried = [feedback[section] for section in range(N_SECTION)]
    kept_hidden = [jnp.zeros((MB, TOKENS, D), jnp.bfloat16) for section in range(N_SECTION)]
    kept_grad = [jnp.zeros((MB, TOKENS, D), jnp.bfloat16) for section in range(N_SECTION)]
    kept_pre = [jnp.zeros((MB, TOKENS, adapter), jnp.bfloat16) for section in range(N_SECTION)]
    kept_act = [jnp.zeros((MB, TOKENS, adapter), jnp.bfloat16) for section in range(N_SECTION)]
    grads_kept = [jnp.zeros((MB, TOKENS, D), jnp.float32) for section in range(N_SECTION)]
    gain_sums = [jnp.zeros((D,), jnp.float32) for section in range(N_SECTION)]
    for slot in range(MB):
        micro = batch_order[slot]
        grad_in = top_grads[micro].astype(jnp.float32)
        for section in reversed(range(N_SECTION)):
            inputs = section_inputs[section][micro]
            grad_out, gain_term, hidden_in, grad_low, grad_pre, active_out = layer_backward(inputs, grad_in, norm_gains[section], weights[section])
            kept_hidden[section] = kept_hidden[section].at[micro].set(hidden_in)
            kept_grad[section] = kept_grad[section].at[micro].set(grad_low)
            kept_pre[section] = kept_pre[section].at[micro].set(grad_pre)
            kept_act[section] = kept_act[section].at[micro].set(active_out)
            grads_kept[section] = grads_kept[section].at[micro].set(grad_out)
            gain_sums[section] = gain_sums[section] + gain_term
            if section > 0:
                carried[section], grad_in = encode(grad_out, carried[section], sign_rows[section], matrix)
    weight_list = []
    for section in range(N_SECTION):
        left_rows = jnp.concatenate([kept_hidden[section].reshape(-1, D), kept_grad[section].reshape(-1, D)], axis=0)
        right_rows = jnp.concatenate([kept_pre[section].reshape(-1, adapter), kept_act[section].reshape(-1, adapter)], axis=0)
        summed = lax.dot_general(left_rows, right_rows, (((0,), (0,)), ((), ())), preferred_element_type=jnp.float32)
        weight_list.append(summed)
    input_grads = jnp.stack(grads_kept, axis=0)
    weight_grads = jnp.stack(weight_list, axis=0)
    gain_grads = jnp.stack(gain_sums, axis=0)
    feedback_out = jnp.stack(carried, axis=0)
    return (input_grads, weight_grads, gain_grads, feedback_out)
```

```python
import functools

import jax
import jax.numpy as jnp
from jax import lax
from jax.experimental import pallas as pl
from jax.experimental.pallas import tpu as pltpu
from jax.sharding import PartitionSpec as P

HB = 256
CHUNK = 32
SLOTS = 4
LANES = 128
GROUP = 4
MESH = pl.DeviceIdType.MESH

eps_norm = 1e-05
eps_scale = 1e-06
f32 = jnp.float32
bf16 = jnp.bfloat16


def hadamard(order_size):
    position = jnp.arange(order_size, dtype=jnp.int32)
    shared_bits = jnp.bitwise_and(position[:, None], position[None, :])
    parity = jnp.zeros((order_size, order_size), jnp.int32)
    for bit_place in range(order_size.bit_length() - 1):
        parity = parity + jnp.bitwise_and(jnp.right_shift(shared_bits, bit_place), 1)
    return (1 - 2 * (parity % 2)).astype(f32) / jnp.sqrt(f32(order_size))


def dot(a, b, ca=1, cb=0):
    return lax.dot_general(a, b, (((ca,), (cb,)), ((), ())), preferred_element_type=f32)


def relay_kernel(
    sections, x, top, weight, gain, signs, matrix, fb_in,
    gout, dw, gsum, fb,
    inbox, outbox, hidden, stage, pre, gp, act, sinv, gacc,
    recv_sem, send_sem, out_sem, fb_sem, top_sem,
):
    sec = lax.axis_index("section")
    rows_all, width = x.shape
    rank = weight.shape[1]
    held = fb.shape[0]
    chunks = rows_all // CHUNK
    last = sections - 1
    barrier = pltpu.get_barrier_semaphore()

    @pl.when(sec < last)
    def _():
        pl.semaphore_signal(barrier, inc=1, device_id={"section": sec + 1}, device_id_type=MESH)

    fb_copy = pltpu.make_async_copy(fb_in, fb, fb_sem)
    fb_copy.start()
    top_copy = pltpu.make_async_copy(top, inbox.at[:, pl.ds(0, width)], top_sem)

    @pl.when(sec == last)
    def _():
        top_copy.start()

    gacc[...] = jnp.zeros_like(gacc)
    wide = 1024

    @pl.loop(0, chunks)
    def _(c):
        rows = pl.ds(pl.multiple_of(c * CHUNK, CHUNK), CHUNK)

        def square(k, acc):
            part = x[rows, pl.ds(pl.multiple_of(k * wide, wide), wide)].astype(f32)
            part = part * part
            for j in range(wide // LANES):
                acc = acc + part[:, j * LANES:(j + 1) * LANES]
            return acc

        acc = lax.fori_loop(0, width // wide, square, jnp.zeros((CHUNK, LANES), f32))
        scale_inv = lax.rsqrt(jnp.sum(acc, axis=-1, keepdims=True) / width + eps_norm)
        sinv[rows, :] = jnp.broadcast_to(scale_inv, (CHUNK, LANES))

        @pl.loop(0, width // wide)
        def _(k):
            cols = pl.ds(pl.multiple_of(k * wide, wide), wide)
            hidden[rows, cols] = (x[rows, cols].astype(f32) * scale_inv * gain[:, cols]).astype(bf16)

    pre[...] = jnp.zeros_like(pre)

    @pl.loop(0, width // wide)
    def _(k):
        cols = pl.ds(pl.multiple_of(k * wide, wide), wide)
        pre[...] += dot(hidden[:, cols], weight[cols, :])

    fb_copy.wait()

    @pl.when(sec == last)
    def _():
        top_copy.wait()

    @pl.when(sec > 0)
    def _():
        pl.semaphore_wait(barrier, 1)

    lane = lax.broadcasted_iota(jnp.int32, (CHUNK, LANES), 1)
    group_wide = GROUP * HB

    def send(c, slot):
        return pltpu.make_async_remote_copy(
            src_ref=outbox.at[slot],
            dst_ref=inbox.at[pl.ds(pl.multiple_of(c * CHUNK, CHUNK), CHUNK)],
            send_sem=send_sem.at[slot],
            recv_sem=recv_sem.at[c],
            device_id={"section": sec - 1},
            device_id_type=MESH,
        )

    def store(c, half):
        return pltpu.make_async_copy(
            stage.at[half],
            gout.at[pl.ds(pl.multiple_of(c * CHUNK, CHUNK), CHUNK)],
            out_sem.at[half],
        )

    @pl.loop(0, chunks)
    def _(c):
        rows = pl.ds(pl.multiple_of(c * CHUNK, CHUNK), CHUNK)
        kept = pl.ds(pl.multiple_of(lax.rem(c * CHUNK, held), CHUNK), CHUNK)
        half = lax.rem(c, 2)
        slot = lax.rem(c, SLOTS)

        @pl.when(c >= 2)
        def _():
            store(c - 2, half).wait()

        @pl.when(sec == last)
        def _():
            @pl.loop(0, width // wide)
            def _(k):
                cols = pl.ds(pl.multiple_of(k * wide, wide), wide)
                stage[half, :, cols] = inbox[rows, cols].astype(f32)

        @pl.when(sec < last)
        def _():
            send(c, slot).wait_recv()
            scales = inbox[rows, pl.ds(width, LANES)].astype(f32)

            @pl.loop(0, width // group_wide)
            def _(k):
                for j in range(GROUP):
                    block = k * GROUP + j
                    cols = pl.ds(pl.multiple_of(block * HB, HB), HB)
                    scale = jnp.sum(jnp.where(lane == block, scales, 0.0), axis=-1, keepdims=True)
                    value = dot(inbox[rows, cols], matrix[...]) * scale * signs[1:2, cols]
                    stage[half, :, cols] = value
                    inbox[rows, cols] = value.astype(bf16)

        def multiply(k, acc):
            cols = pl.ds(pl.multiple_of(k * wide, wide), wide)
            return acc + dot(inbox[rows, cols], weight[cols, :])

        grad_act = lax.fori_loop(0, width // wide, multiply, jnp.zeros((CHUNK, rank), f32))
        pre_here = pre[rows, :]
        sigma = jax.nn.sigmoid(pre_here)
        act[rows, :] = (pre_here * sigma).astype(bf16)
        grad_pre = (grad_act * sigma * (1.0 + pre_here * (1.0 - sigma))).astype(bf16)
        gp[rows, :] = grad_pre
        inner = jnp.sum(grad_pre.astype(f32) * pre_here, axis=-1, keepdims=True) / width
        scale_inv = sinv[rows, 0:1]

        def layer_block(cols):
            grad_hidden = dot(grad_pre, weight[cols, :], 1, 1)
            normed = x[rows, cols].astype(f32) * scale_inv
            term = grad_hidden * normed
            total = term[0:8]
            for j in range(1, CHUNK // 8):
                total = total + term[8 * j:8 * j + 8]
            gacc[:, cols] += total
            grad_out = stage[half, :, cols] + scale_inv * (grad_hidden * gain[:, cols] - normed * inner)
            stage[half, :, cols] = grad_out
            return grad_out

        @pl.when(sec == 0)
        def _():
            @pl.loop(0, width // group_wide)
            def _(k):
                for j in range(GROUP):
                    layer_block(pl.ds(pl.multiple_of((k * GROUP + j) * HB, HB), HB))

        @pl.when(sec > 0)
        def _():
            @pl.when(c >= SLOTS)
            def _():
                send(c - SLOTS, slot).wait_send()

            def encode(k, scales):
                for j in range(GROUP):
                    block = k * GROUP + j
                    cols = pl.ds(pl.multiple_of(block * HB, HB), HB)
                    value = layer_block(cols) + fb[kept, cols]
                    sign = signs[0:1, cols]
                    turned = value * sign
                    high = turned.astype(bf16)
                    low = (turned - high.astype(f32)).astype(bf16)
                    rotated = dot(high, matrix[...]) + dot(low, matrix[...])
                    scale = jnp.sum(jnp.abs(rotated), axis=-1, keepdims=True) / HB + eps_scale
                    scale = scale.astype(bf16).astype(f32)
                    levels = jnp.clip(rotated * (1.0 / scale), -1.0, 1.0).astype(bf16)
                    outbox[slot, :, cols] = levels
                    fb[kept, cols] = value - dot(levels, matrix[...]) * scale * sign
                    scales = jnp.where(lane == block, scale, scales)
                return scales

            scales = lax.fori_loop(0, width // group_wide, encode, jnp.zeros((CHUNK, LANES), f32))
            outbox[slot, :, pl.ds(width, LANES)] = scales.astype(bf16)
            send(c, slot).start()

        store(c, half).start()

    @pl.loop(0, width // HB)
    def _(k):
        cols = pl.ds(pl.multiple_of(k * HB, HB), HB)
        dw[cols, :] = (dot(hidden[:, cols], gp[...], 0, 0) + dot(inbox[:, pl.ds(pl.multiple_of(k * HB, HB), HB)], act[...], 0, 0)).astype(dw.dtype)

    gsum[...] = jnp.sum(gacc[...], axis=0, keepdims=True)
    for c in range(max(0, chunks - 2), chunks):
        store(c, c % 2).wait()

    @pl.when(sec > 0)
    def _():
        for c in range(max(0, chunks - SLOTS), chunks):
            send(c, c % SLOTS).wait_send()


def per_device(
    section_inputs, top_grads, weights, norm_gains, feedback, rotation_bits, batch_order
):
    section_count = lax.axis_size("section")
    section_here = lax.axis_index("section")
    micro_count, token_count, width = section_inputs.shape[1:]
    rank = weights.shape[2]
    rows = micro_count * token_count
    chunks = rows // CHUNK
    weight = lax.all_gather(weights[0], "fsdp", axis=0, tiled=True)
    gain_row = lax.all_gather(norm_gains, "fsdp", axis=1, tiled=True)
    above = jnp.minimum(section_here + 1, section_count - 1)
    bits = jnp.stack([rotation_bits[section_here], rotation_bits[above]])
    signs = (1 - 2 * bits).astype(f32)
    x = section_inputs[0][batch_order].reshape(rows, width)
    top = top_grads[batch_order].reshape(rows, width)
    vmem = pl.BlockSpec(memory_space=pltpu.VMEM)
    hbm = pl.BlockSpec(memory_space=pl.ANY)
    gout, dw, gsum, fb_out = pl.pallas_call(
        functools.partial(relay_kernel, section_count),
        out_shape=(
            jax.ShapeDtypeStruct((rows, width), f32),
            jax.ShapeDtypeStruct((width, rank), bf16),
            jax.ShapeDtypeStruct((1, width), f32),
            jax.ShapeDtypeStruct((token_count, width), f32),
        ),
        in_specs=[vmem, hbm, vmem, vmem, vmem, vmem, hbm],
        out_specs=(hbm, vmem, vmem, vmem),
        scratch_shapes=[
            pltpu.VMEM((rows, width + LANES), bf16),
            pltpu.VMEM((SLOTS, CHUNK, width + LANES), bf16),
            pltpu.VMEM((rows, width), bf16),
            pltpu.VMEM((2, CHUNK, width), f32),
            pltpu.VMEM((rows, rank), f32),
            pltpu.VMEM((rows, rank), bf16),
            pltpu.VMEM((rows, rank), bf16),
            pltpu.VMEM((rows, LANES), f32),
            pltpu.VMEM((8, width), f32),
            pltpu.SemaphoreType.DMA((chunks,)),
            pltpu.SemaphoreType.DMA((SLOTS,)),
            pltpu.SemaphoreType.DMA((2,)),
            pltpu.SemaphoreType.DMA,
            pltpu.SemaphoreType.DMA,
        ],
        compiler_params=pltpu.CompilerParams(
            collective_id=0, has_side_effects=True, vmem_limit_bytes=60 * 1024 * 1024
        ),
    )(x, top, weight, gain_row, signs, hadamard(HB).astype(bf16), feedback[0])
    gain_share = lax.psum_scatter(gsum, "fsdp", scatter_dimension=1, tiled=True)
    weight_share = lax.psum_scatter(dw, "fsdp", scatter_dimension=0, tiled=True).astype(f32)
    slot_of = jnp.argmax(batch_order[None, :] == jnp.arange(micro_count)[:, None], axis=1)
    input_grads = gout.reshape(micro_count, token_count, width)[slot_of]
    return (input_grads[None], weight_share[None], gain_share, fb_out[None])


def solution(mesh):
    return jax.shard_map(
        per_device,
        mesh=mesh,
        in_specs=(
            P("section", None, "fsdp", None),
            P(None, "fsdp", None),
            P("section", "fsdp", None),
            P("section", "fsdp"),
            P("section", "fsdp", None),
            P(),
            P(),
        ),
        out_specs=(
            P("section", None, "fsdp", None),
            P("section", "fsdp", None),
            P("section", "fsdp"),
            P("section", "fsdp", None),
        ),
        check_vma=False,
    )
```

```python
import functools

import jax
import jax.numpy as jnp
from jax import lax
from jax.experimental import pallas as pl
from jax.experimental.pallas import tpu as pltpu
from jax.sharding import PartitionSpec as P

HB = 256
CHUNK = 32
SLOTS = 4
LANES = 128
GROUP = 8
MESH = pl.DeviceIdType.MESH

eps_norm = 1e-05
eps_scale = 1e-06
f32 = jnp.float32
bf16 = jnp.bfloat16


def hadamard(order_size):
    position = jnp.arange(order_size, dtype=jnp.int32)
    shared_bits = jnp.bitwise_and(position[:, None], position[None, :])
    parity = jnp.zeros((order_size, order_size), jnp.int32)
    for bit_place in range(order_size.bit_length() - 1):
        parity = parity + jnp.bitwise_and(jnp.right_shift(shared_bits, bit_place), 1)
    return (1 - 2 * (parity % 2)).astype(f32) / jnp.sqrt(f32(order_size))


def dot(a, b, ca=1, cb=0):
    return lax.dot_general(a, b, (((ca,), (cb,)), ((), ())), preferred_element_type=f32)


def stack(value):
    return jnp.concatenate(
        [value[:, j * HB:(j + 1) * HB] for j in range(value.shape[1] // HB)], axis=0
    )


def unstack(value, rows):
    return jnp.concatenate(
        [value[j * rows:(j + 1) * rows] for j in range(value.shape[0] // rows)], axis=1
    )


def span(index, size):
    return pl.ds(pl.multiple_of(index * size, size), size)


def relay_kernel(
    sections, peers, x, top, weight_in, gain_in, signs, matrix, fb_in,
    gout, dw, gain_out, fb,
    weight, gain, inbox, outbox, hidden, stage, pre, grad_act, right, sinv, gacc,
    gsum, gparts, own_part, sib_out, sib_in, chain_in,
    recv_sem, send_sem, out_sem, fb_sem, top_sem, own_sem,
    w_recv, w_send, g_recv, g_send, s_recv, s_send, b_recv, b_send, c_recv, c_send,
):
    sec = lax.axis_index("section")
    here = lax.axis_index("fsdp")
    chips = peers // 2
    chip = here // 2
    core = lax.rem(here, 2)
    sibling = here + 1 - 2 * core
    rows_all, width = x.shape
    rank = weight.shape[1]
    shard = width // peers
    held = fb.shape[0]
    chunks = rows_all // CHUNK
    last = sections - 1
    wide = 1024
    barrier = pltpu.get_barrier_semaphore()

    for k in range(1, peers):
        pl.semaphore_signal(
            barrier, inc=1, device_id={"fsdp": lax.rem(here + k, peers)}, device_id_type=MESH
        )

    @pl.when(sec < last)
    def _():
        pl.semaphore_signal(barrier, inc=1, device_id={"section": sec + 1}, device_id_type=MESH)

    own_copy = pltpu.make_async_copy(weight_in, weight.at[span(here, shard)], own_sem)
    own_copy.start()
    fb_copy = pltpu.make_async_copy(fb_in, fb, fb_sem)
    fb_copy.start()
    top_copy = pltpu.make_async_copy(top, inbox.at[:, pl.ds(0, width)], top_sem)

    @pl.when(sec == last)
    def _():
        top_copy.start()

    gain[:, span(here, shard)] = gain_in[...]
    gacc[...] = jnp.zeros_like(gacc)
    pre[...] = jnp.zeros_like(pre)
    pl.semaphore_wait(barrier, peers - 1 + (sec > 0).astype(jnp.int32))

    own_copy.wait()

    def weight_copy(owner, target, way):
        return pltpu.make_async_remote_copy(
            src_ref=weight.at[span(owner, shard)],
            dst_ref=weight.at[span(owner, shard)],
            send_sem=w_send.at[way * chips + owner // 2],
            recv_sem=w_recv.at[owner],
            device_id={"fsdp": target},
            device_id_type=MESH,
        )

    def pass_right(owner, act):
        @pl.when(chip < chips - 1)
        def _():
            act(weight_copy(owner, here + 2, 0))

    def pass_left(owner, act):
        @pl.when(chip > 0)
        def _():
            act(weight_copy(owner, here - 2, 1))

    def pass_sibling(owner, act):
        act(weight_copy(owner, sibling, 2))

    def start(copy):
        copy.start()

    def finish(copy):
        copy.wait_send()

    def gain_copy(k):
        return pltpu.make_async_remote_copy(
            src_ref=gain.at[:, span(here, shard)],
            dst_ref=gain.at[:, span(here, shard)],
            send_sem=g_send.at[k],
            recv_sem=g_recv.at[k],
            device_id={"fsdp": lax.rem(here + k, peers)},
            device_id_type=MESH,
        )

    for k in range(1, peers):
        gain_copy(k).start()
    pass_right(here, start)
    pass_left(here, start)
    pass_sibling(here, start)

    @pl.loop(0, chunks)
    def _(c):
        rows = span(c, CHUNK)

        def square(k, acc):
            part = x[rows, span(k, wide)].astype(f32)
            part = part * part
            for j in range(wide // LANES):
                acc = acc + part[:, j * LANES:(j + 1) * LANES]
            return acc

        acc = lax.fori_loop(0, width // wide, square, jnp.zeros((CHUNK, LANES), f32))
        scale_inv = lax.rsqrt(jnp.sum(acc, axis=-1, keepdims=True) / width + eps_norm)
        sinv[rows, :] = jnp.broadcast_to(scale_inv, (CHUNK, LANES))

    for k in range(1, peers):
        pltpu.make_async_remote_copy(
            src_ref=gain.at[:, span(here, shard)],
            dst_ref=gain.at[:, span(lax.rem(here + peers - k, peers), shard)],
            send_sem=g_send.at[k],
            recv_sem=g_recv.at[k],
            device_id={"fsdp": lax.rem(here + k, peers)},
            device_id_type=MESH,
        ).wait_recv()

    @pl.loop(0, chunks)
    def _(c):
        rows = span(c, CHUNK)
        scale_inv = sinv[rows, 0:1]

        @pl.loop(0, width // wide)
        def _(k):
            cols = span(k, wide)
            hidden[rows, cols] = (x[rows, cols].astype(f32) * scale_inv * gain[:, cols]).astype(bf16)

    def accumulate(spot):
        other = spot * 2 + 1 - core
        weight_copy(other, sibling, 2).wait_recv()
        for owner in (spot * 2 + core, other):
            cols = span(owner, shard)
            pre[...] += dot(hidden[:, cols], weight[cols, :])

    def accumulate_around(distance):
        @pl.when(chip >= distance)
        def _():
            accumulate(chip - distance)

        if distance > 0:
            @pl.when(chip + distance < chips)
            def _():
                accumulate(chip + distance)

    for distance in range(1, chips):
        @pl.when(chip >= distance)
        def _():
            owner = here - 2 * distance
            weight_copy(owner, sibling, 2).wait_recv()
            pass_right(owner, start)
            pass_sibling(owner, start)

        @pl.when(chip + distance < chips)
        def _():
            owner = here + 2 * distance
            weight_copy(owner, sibling, 2).wait_recv()
            pass_left(owner, start)
            pass_sibling(owner, start)

        accumulate_around(distance - 1)
    accumulate_around(chips - 1)

    fb_copy.wait()

    @pl.when(sec == last)
    def _():
        top_copy.wait()

    lane = lax.broadcasted_iota(jnp.int32, (CHUNK, LANES), 1)
    group_wide = GROUP * HB
    groups = width // group_wide

    def send(c, slot):
        return pltpu.make_async_remote_copy(
            src_ref=outbox.at[slot],
            dst_ref=inbox.at[span(c, CHUNK)],
            send_sem=send_sem.at[slot],
            recv_sem=recv_sem.at[c],
            device_id={"section": sec - 1},
            device_id_type=MESH,
        )

    def store(c, half):
        return pltpu.make_async_copy(stage.at[half], gout.at[span(c, CHUNK)], out_sem.at[half])

    @pl.loop(0, chunks)
    def _(c):
        rows = span(c, CHUNK)
        kept = span(lax.rem(c, held // CHUNK), CHUNK)
        half = lax.rem(c, 2)
        slot = lax.rem(c, SLOTS)

        @pl.when(c >= 2)
        def _():
            store(c - 2, half).wait()

        @pl.when(sec == last)
        def _():
            def multiply(k, acc):
                cols = span(k, group_wide)
                value = inbox[rows, cols]
                stage[half, :, cols] = value.astype(f32)
                return acc + dot(value, weight[cols, :])

            grad_act[...] = lax.fori_loop(0, groups, multiply, jnp.zeros((CHUNK, rank), f32))

        @pl.when(sec < last)
        def _():
            send(c, slot).wait_recv()
            scales = inbox[rows, pl.ds(width, LANES)].astype(f32)

            def decode(k, acc):
                cols = span(k, group_wide)
                scale = jnp.concatenate([
                    jnp.sum(jnp.where(lane == k * GROUP + j, scales, 0.0), axis=-1, keepdims=True)
                    for j in range(GROUP)
                ], axis=0)
                value = dot(stack(inbox[rows, cols]), matrix[...]) * scale
                value = unstack(value, CHUNK) * signs[1:2, cols]
                low = value.astype(bf16)
                stage[half, :, cols] = value
                inbox[rows, cols] = low
                return acc + dot(low, weight[cols, :])

            grad_act[...] = lax.fori_loop(0, groups, decode, jnp.zeros((CHUNK, rank), f32))

        pre_here = pre[rows, :]
        sigma = jax.nn.sigmoid(pre_here)
        grad_pre = (grad_act[...] * sigma * (1.0 + pre_here * (1.0 - sigma))).astype(bf16)
        right[rows, :] = grad_pre
        right[span(c + chunks, CHUNK), :] = (pre_here * sigma).astype(bf16)
        inner = jnp.sum(grad_pre.astype(f32) * pre_here, axis=-1, keepdims=True) / width
        scale_inv = sinv[rows, 0:1]

        def layer_block(cols):
            grad_hidden = dot(grad_pre, weight[cols, :], 1, 1)
            normed = x[rows, cols].astype(f32) * scale_inv
            term = grad_hidden * normed
            total = term[0:8]
            for j in range(1, CHUNK // 8):
                total = total + term[8 * j:8 * j + 8]
            grad_out = stage[half, :, cols] + scale_inv * (grad_hidden * gain[:, cols] - normed * inner)
            return total, grad_out

        @pl.when(sec == 0)
        def _():
            @pl.loop(0, groups)
            def _(k):
                cols = span(k, group_wide)
                total, grad_out = layer_block(cols)
                gacc[:, cols] += total
                stage[half, :, cols] = grad_out

        @pl.when(sec > 0)
        def _():
            @pl.when(c >= SLOTS)
            def _():
                send(c - SLOTS, slot).wait_send()

            def encode(k, scales):
                cols = span(k, group_wide)
                total, grad_out = layer_block(cols)
                value = grad_out + fb[kept, cols]
                sign = signs[0:1, cols]
                turned = stack(value * sign)
                high = turned.astype(bf16)
                low = (turned - high.astype(f32)).astype(bf16)
                rotated = dot(jnp.concatenate([high, low], axis=0), matrix[...])
                rotated = rotated[:GROUP * CHUNK] + rotated[GROUP * CHUNK:]
                scale = jnp.sum(jnp.abs(rotated), axis=-1, keepdims=True) / HB + eps_scale
                scale = scale.astype(bf16).astype(f32)
                levels = jnp.clip(rotated * (1.0 / scale), -1.0, 1.0).astype(bf16)
                decoded = unstack(dot(levels, matrix[...]) * scale, CHUNK) * sign
                gacc[:, cols] += total
                stage[half, :, cols] = grad_out
                outbox[slot, :, cols] = unstack(levels, CHUNK)
                fb[kept, cols] = value - decoded
                for j in range(GROUP):
                    scales = jnp.where(
                        lane == k * GROUP + j, scale[j * CHUNK:(j + 1) * CHUNK], scales
                    )
                return scales

            scales = lax.fori_loop(0, groups, encode, jnp.zeros((CHUNK, LANES), f32))
            outbox[slot, :, pl.ds(width, LANES)] = scales.astype(bf16)
            send(c, slot).start()

        store(c, half).start()

    gsum[...] = jnp.sum(gacc[...], axis=0, keepdims=True)

    def sum_copy(k):
        target = lax.rem(here + k, peers)
        return pltpu.make_async_remote_copy(
            src_ref=gsum.at[:, span(target, shard)],
            dst_ref=gparts.at[k],
            send_sem=s_send.at[k],
            recv_sem=s_recv.at[k],
            device_id={"fsdp": target},
            device_id_type=MESH,
        )

    for k in range(1, peers):
        sum_copy(k).start()

    piece = 256

    def share(owner, into, spot):
        @pl.loop(0, shard // piece)
        def _(k):
            cols = pl.ds(pl.multiple_of(owner * shard + k * piece, piece), piece)
            left = jnp.concatenate([hidden[:, cols], inbox[:, cols]], axis=0)
            into[spot, span(k, piece), :] = dot(left, right[...], 0, 0).astype(bf16)

    def sibling_copy(spot):
        return pltpu.make_async_remote_copy(
            src_ref=sib_out.at[spot],
            dst_ref=sib_in.at[spot],
            send_sem=b_send.at[spot],
            recv_sem=b_recv.at[spot],
            device_id={"fsdp": sibling},
            device_id_type=MESH,
        )

    @pl.loop(0, chips)
    def _(k):
        low_half = (chip < chips // 2).astype(jnp.int32)
        spot = low_half * (chips - 1 - k) + (1 - low_half) * k
        share(spot * 2 + 1 - core, sib_out, spot)
        sibling_copy(spot).start()
        share(spot * 2 + core, own_part, spot)

    def chain_copy(spot, way):
        arrive = spot
        target = here + 2
        if way == 1:
            target = here - 2
            arrive = spot + (chips - spot) * (chip - 1 == spot).astype(jnp.int32)
        return pltpu.make_async_remote_copy(
            src_ref=own_part.at[spot],
            dst_ref=chain_in.at[arrive],
            send_sem=c_send.at[spot],
            recv_sem=c_recv.at[arrive],
            device_id={"fsdp": target},
            device_id_type=MESH,
        )

    def arrived(slot):
        pltpu.make_async_remote_copy(
            src_ref=own_part.at[0],
            dst_ref=chain_in.at[slot],
            send_sem=c_send.at[0],
            recv_sem=c_recv.at[slot],
            device_id={"fsdp": sibling},
            device_id_type=MESH,
        ).wait_recv()

    def merge(spot, inner_chip):
        sibling_copy(spot).wait_recv()

        @pl.when(inner_chip)
        def _():
            arrived(spot)

            @pl.loop(0, shard // piece)
            def _(k):
                part = span(k, piece)
                own_part[spot, part, :] = (
                    own_part[spot, part, :].astype(f32) + sib_in[spot, part, :].astype(f32)
                    + chain_in[spot, part, :].astype(f32)
                ).astype(bf16)

        @pl.when(jnp.logical_not(inner_chip))
        def _():
            @pl.loop(0, shard // piece)
            def _(k):
                part = span(k, piece)
                own_part[spot, part, :] = (
                    own_part[spot, part, :].astype(f32) + sib_in[spot, part, :].astype(f32)
                ).astype(bf16)

    def go_right(k):
        spot = chips - 1 - k

        @pl.when(spot > chip)
        def _():
            merge(spot, chip > 0)
            chain_copy(spot, 0).start()

    def go_left(k):
        @pl.when(k < chip)
        def _():
            merge(k, chip < chips - 1)
            chain_copy(k, 1).start()

    @pl.loop(0, chips)
    def _(k):
        @pl.when(chip < chips // 2)
        def _():
            go_right(k)
            go_left(k)

        @pl.when(chip >= chips // 2)
        def _():
            go_left(k)
            go_right(k)

    sibling_copy(chip).wait_recv()

    @pl.loop(0, shard // piece)
    def _(k):
        part = span(k, piece)
        dw[part, :] = own_part[chip, part, :].astype(f32) + sib_in[chip, part, :].astype(f32)

    def add_arrived(slot):
        arrived(slot)

        @pl.loop(0, shard // piece)
        def _(k):
            part = span(k, piece)
            dw[part, :] += chain_in[slot, part, :].astype(f32)

    @pl.when(chip > 0)
    def _():
        add_arrived(chip)

    @pl.when(chip < chips - 1)
    def _():
        add_arrived(chips)

    total = gsum[:, span(here, shard)]
    for k in range(1, peers):
        sum_copy(k).wait_recv()
        total = total + gparts[k]
    gain_out[...] = total

    for c in range(max(0, chunks - 2), chunks):
        store(c, c % 2).wait()

    @pl.when(sec > 0)
    def _():
        for c in range(max(0, chunks - SLOTS), chunks):
            send(c, c % SLOTS).wait_send()

    for k in range(1, peers):
        gain_copy(k).wait_send()
        sum_copy(k).wait_send()
    pass_right(here, finish)
    pass_left(here, finish)
    pass_sibling(here, finish)
    for distance in range(1, chips):
        @pl.when(chip >= distance)
        def _():
            pass_right(here - 2 * distance, finish)
            pass_sibling(here - 2 * distance, finish)

        @pl.when(chip + distance < chips)
        def _():
            pass_left(here + 2 * distance, finish)
            pass_sibling(here + 2 * distance, finish)

    @pl.loop(0, chips)
    def _(k):
        sibling_copy(k).wait_send()

        @pl.when(k > chip)
        def _():
            chain_copy(k, 0).wait_send()

        @pl.when(k < chip)
        def _():
            chain_copy(k, 1).wait_send()


def reorder_kernel(scatter, order, *refs):
    count = (len(refs) - 1) // 2
    sem = refs[-1]
    copies = []
    for i in range(count):
        source, target = refs[i], refs[count + i]
        pieces = 4
        rows = source.shape[1] // pieces
        for m in range(source.shape[0]):
            for j in range(pieces):
                part = pl.ds(j * rows, rows)
                a, b = (m, order[m]) if scatter else (order[m], m)
                copies.append(
                    pltpu.make_async_copy(source.at[a, part], target.at[b, part], sem.at[len(copies)])
                )
    for copy in copies:
        copy.start()
    for copy in copies:
        copy.wait()


def reorder(order, arrays, scatter):
    hbm = pl.BlockSpec(memory_space=pl.ANY)
    return pl.pallas_call(
        functools.partial(reorder_kernel, scatter),
        out_shape=tuple(jax.ShapeDtypeStruct(a.shape, a.dtype) for a in arrays),
        in_specs=[pl.BlockSpec(memory_space=pltpu.SMEM)] + [hbm] * len(arrays),
        out_specs=(hbm,) * len(arrays),
        scratch_shapes=[pltpu.SemaphoreType.DMA((4 * len(arrays) * arrays[0].shape[0],))],
    )(order, *arrays)


def per_device(
    section_inputs, top_grads, weights, norm_gains, feedback, rotation_bits, batch_order
):
    section_count = lax.axis_size("section")
    peers = lax.axis_size("fsdp")
    section_here = lax.axis_index("section")
    micro_count, token_count, width = section_inputs.shape[1:]
    shard, rank = weights.shape[1:]
    rows = micro_count * token_count
    chunks = rows // CHUNK
    chips = peers // 2
    above = jnp.minimum(section_here + 1, section_count - 1)
    bits = jnp.stack([rotation_bits[section_here], rotation_bits[above]])
    signs = (1 - 2 * bits).astype(f32)
    x, top = reorder(batch_order, (section_inputs[0], top_grads), False)
    vmem = pl.BlockSpec(memory_space=pltpu.VMEM)
    hbm = pl.BlockSpec(memory_space=pl.ANY)
    dma = pltpu.SemaphoreType.DMA
    gout, dw, gain_share, fb_out = pl.pallas_call(
        functools.partial(relay_kernel, section_count, peers),
        out_shape=(
            jax.ShapeDtypeStruct((rows, width), f32),
            jax.ShapeDtypeStruct((shard, rank), f32),
            jax.ShapeDtypeStruct((1, shard), f32),
            jax.ShapeDtypeStruct((token_count, width), f32),
        ),
        in_specs=[vmem, hbm, hbm, vmem, vmem, vmem, hbm],
        out_specs=(hbm, vmem, vmem, vmem),
        scratch_shapes=[
            pltpu.VMEM((width, rank), bf16),
            pltpu.VMEM((1, width), f32),
            pltpu.VMEM((rows, width + LANES), bf16),
            pltpu.VMEM((SLOTS, CHUNK, width + LANES), bf16),
            pltpu.VMEM((rows, width), bf16),
            pltpu.VMEM((2, CHUNK, width), f32),
            pltpu.VMEM((rows, rank), f32),
            pltpu.VMEM((CHUNK, rank), f32),
            pltpu.VMEM((2 * rows, rank), bf16),
            pltpu.VMEM((rows, LANES), f32),
            pltpu.VMEM((8, width), f32),
            pltpu.VMEM((1, width), f32),
            pltpu.VMEM((peers, 1, shard), f32),
            pltpu.VMEM((chips, shard, rank), bf16),
            pltpu.VMEM((chips, shard, rank), bf16),
            pltpu.VMEM((chips, shard, rank), bf16),
            pltpu.VMEM((chips + 1, shard, rank), bf16),
            dma((chunks,)), dma((SLOTS,)), dma((2,)), dma, dma, dma,
            dma((peers,)), dma((3 * chips,)),
            dma((peers,)), dma((peers,)),
            dma((peers,)), dma((peers,)),
            dma((chips,)), dma((chips,)),
            dma((chips + 1,)), dma((chips,)),
        ],
        compiler_params=pltpu.CompilerParams(
            collective_id=0, has_side_effects=True, vmem_limit_bytes=60 * 1024 * 1024
        ),
    )(
        x.reshape(rows, width), top.reshape(rows, width), weights[0], norm_gains, signs,
        hadamard(HB).astype(bf16), feedback[0],
    )
    (input_grads,) = reorder(batch_order, (gout.reshape(micro_count, token_count, width),), True)
    return (input_grads[None], dw[None], gain_share, fb_out[None])


def solution(mesh):
    return jax.shard_map(
        per_device,
        mesh=mesh,
        in_specs=(
            P("section", None, "fsdp", None),
            P(None, "fsdp", None),
            P("section", "fsdp", None),
            P("section", "fsdp"),
            P("section", "fsdp", None),
            P(),
            P(),
        ),
        out_specs=(
            P("section", None, "fsdp", None),
            P("section", "fsdp", None),
            P("section", "fsdp"),
            P("section", "fsdp", None),
        ),
        check_vma=False,
    )
```

```python
import functools

import jax
import jax.numpy as jnp
from jax import lax
from jax.experimental import pallas as pl
from jax.experimental.pallas import tpu as pltpu
from jax.sharding import PartitionSpec as P

HB = 256
CHUNK = 32
SLOTS = 4
LANES = 128
GROUP = 8
MESH = pl.DeviceIdType.MESH

eps_norm = 1e-05
eps_scale = 1e-06
f32 = jnp.float32
bf16 = jnp.bfloat16


def hadamard(order_size):
    position = jnp.arange(order_size, dtype=jnp.int32)
    shared_bits = jnp.bitwise_and(position[:, None], position[None, :])
    parity = jnp.zeros((order_size, order_size), jnp.int32)
    for bit_place in range(order_size.bit_length() - 1):
        parity = parity + jnp.bitwise_and(jnp.right_shift(shared_bits, bit_place), 1)
    return (1 - 2 * (parity % 2)).astype(f32) / jnp.sqrt(f32(order_size))


def dot(a, b, ca=1, cb=0):
    return lax.dot_general(a, b, (((ca,), (cb,)), ((), ())), preferred_element_type=f32)


def stack(value):
    return jnp.concatenate(
        [value[:, j * HB:(j + 1) * HB] for j in range(value.shape[1] // HB)], axis=0
    )


def unstack(value, rows):
    return jnp.concatenate(
        [value[j * rows:(j + 1) * rows] for j in range(value.shape[0] // rows)], axis=1
    )


def span(index, size):
    return pl.ds(pl.multiple_of(index * size, size), size)


def relay_kernel(
    sections, peers, x, top, weight_in, gain_in, signs, matrix, fb_in,
    gout, dw, gain_out, fb,
    weight, gain, inbox, outbox, hidden, stage, pre, grad_act, right, sinv, gacc,
    gsum, gparts, own_part, sib_out, sib_in, chain_in,
    recv_sem, send_sem, out_sem, fb_sem, top_sem, own_sem,
    w_recv, w_send, g_recv, g_send, s_recv, s_send, b_recv, b_send, c_recv, c_send,
):
    sec = lax.axis_index("section")
    here = lax.axis_index("fsdp")
    chips = peers // 2
    chip = here // 2
    core = lax.rem(here, 2)
    sibling = here + 1 - 2 * core
    rows_all, width = x.shape
    rank = weight.shape[1]
    shard = width // peers
    held = fb.shape[0]
    chunks = rows_all // CHUNK
    last = sections - 1
    wide = 1024
    barrier = pltpu.get_barrier_semaphore()

    for k in range(1, peers):
        pl.semaphore_signal(
            barrier, inc=1, device_id={"fsdp": lax.rem(here + k, peers)}, device_id_type=MESH
        )

    @pl.when(sec < last)
    def _():
        pl.semaphore_signal(barrier, inc=1, device_id={"section": sec + 1}, device_id_type=MESH)

    own_copy = pltpu.make_async_copy(weight_in, weight.at[span(here, shard)], own_sem)
    own_copy.start()
    fb_copy = pltpu.make_async_copy(fb_in, fb, fb_sem)
    fb_copy.start()
    group_wide = GROUP * HB
    groups = width // group_wide
    top_copies = [
        pltpu.make_async_copy(
            top.at[:, pl.ds(k * group_wide, group_wide)],
            inbox.at[k, :, pl.ds(0, group_wide)],
            top_sem.at[k],
        )
        for k in range(groups)
    ]

    @pl.when(sec == last)
    def _():
        for copy in top_copies:
            copy.start()

    gain[:, span(here, shard)] = gain_in[...]
    gacc[...] = jnp.zeros_like(gacc)
    pre[...] = jnp.zeros_like(pre)
    grad_act[...] = jnp.zeros_like(grad_act)
    pl.semaphore_wait(barrier, peers - 1 + (sec > 0).astype(jnp.int32))

    own_copy.wait()

    def weight_copy(owner, target, way):
        return pltpu.make_async_remote_copy(
            src_ref=weight.at[span(owner, shard)],
            dst_ref=weight.at[span(owner, shard)],
            send_sem=w_send.at[way * chips + owner // 2],
            recv_sem=w_recv.at[owner],
            device_id={"fsdp": target},
            device_id_type=MESH,
        )

    def pass_right(owner, act):
        @pl.when(chip < chips - 1)
        def _():
            act(weight_copy(owner, here + 2, 0))

    def pass_left(owner, act):
        @pl.when(chip > 0)
        def _():
            act(weight_copy(owner, here - 2, 1))

    def pass_sibling(owner, act):
        act(weight_copy(owner, sibling, 2))

    def start(copy):
        copy.start()

    def finish(copy):
        copy.wait_send()

    def gain_copy(k):
        return pltpu.make_async_remote_copy(
            src_ref=gain.at[:, span(here, shard)],
            dst_ref=gain.at[:, span(here, shard)],
            send_sem=g_send.at[k],
            recv_sem=g_recv.at[k],
            device_id={"fsdp": lax.rem(here + k, peers)},
            device_id_type=MESH,
        )

    for k in range(1, peers):
        gain_copy(k).start()
    pass_right(here, start)
    pass_left(here, start)
    pass_sibling(here, start)

    @pl.loop(0, chunks)
    def _(c):
        rows = span(c, CHUNK)

        def square(k, acc):
            part = x[rows, span(k, wide)].astype(f32)
            part = part * part
            for j in range(wide // LANES):
                acc = acc + part[:, j * LANES:(j + 1) * LANES]
            return acc

        acc = lax.fori_loop(0, width // wide, square, jnp.zeros((CHUNK, LANES), f32))
        scale_inv = lax.rsqrt(jnp.sum(acc, axis=-1, keepdims=True) / width + eps_norm)
        sinv[rows, :] = jnp.broadcast_to(scale_inv, (CHUNK, LANES))

    for k in range(1, peers):
        pltpu.make_async_remote_copy(
            src_ref=gain.at[:, span(here, shard)],
            dst_ref=gain.at[:, span(lax.rem(here + peers - k, peers), shard)],
            send_sem=g_send.at[k],
            recv_sem=g_recv.at[k],
            device_id={"fsdp": lax.rem(here + k, peers)},
            device_id_type=MESH,
        ).wait_recv()

    @pl.loop(0, chunks)
    def _(c):
        rows = span(c, CHUNK)
        scale_inv = sinv[rows, 0:1]

        @pl.loop(0, width // wide)
        def _(k):
            cols = span(k, wide)
            hidden[rows, cols] = (x[rows, cols].astype(f32) * scale_inv * gain[:, cols]).astype(bf16)

    @pl.when(sec == last)
    def _():
        for copy in top_copies:
            copy.wait()

    def accumulate(spot):
        other = spot * 2 + 1 - core
        weight_copy(other, sibling, 2).wait_recv()
        for owner in (spot * 2 + core, other):
            cols = span(owner, shard)
            pre[...] += dot(hidden[:, cols], weight[cols, :])

            @pl.when(sec == last)
            def _():
                first = owner * shard
                part = pl.ds(pl.multiple_of(lax.rem(first, group_wide), shard), shard)
                grad_act[...] += dot(inbox[first // group_wide, :, part], weight[cols, :])

    def accumulate_around(distance):
        @pl.when(chip >= distance)
        def _():
            accumulate(chip - distance)

        if distance > 0:
            @pl.when(chip + distance < chips)
            def _():
                accumulate(chip + distance)

    for distance in range(1, chips):
        @pl.when(chip >= distance)
        def _():
            owner = here - 2 * distance
            weight_copy(owner, sibling, 2).wait_recv()
            pass_right(owner, start)
            pass_sibling(owner, start)

        @pl.when(chip + distance < chips)
        def _():
            owner = here + 2 * distance
            weight_copy(owner, sibling, 2).wait_recv()
            pass_left(owner, start)
            pass_sibling(owner, start)

        accumulate_around(distance - 1)
    accumulate_around(chips - 1)

    fb_copy.wait()
    lane = lax.broadcasted_iota(jnp.int32, (CHUNK, LANES), 1)

    def send(c, slot, k):
        return pltpu.make_async_remote_copy(
            src_ref=outbox.at[slot, k],
            dst_ref=inbox.at[k, span(c, CHUNK)],
            send_sem=send_sem.at[slot, k],
            recv_sem=recv_sem.at[c, k],
            device_id={"section": sec - 1},
            device_id_type=MESH,
        )

    def store(c, half):
        return pltpu.make_async_copy(stage.at[half], gout.at[span(c, CHUNK)], out_sem.at[half])

    @pl.loop(0, chunks)
    def _(c):
        rows = span(c, CHUNK)
        kept = span(lax.rem(c, held // CHUNK), CHUNK)
        half = lax.rem(c, 2)
        slot = lax.rem(c, SLOTS)

        @pl.when(c >= 2)
        def _():
            store(c - 2, half).wait()

        @pl.when(sec == last)
        def _():
            @pl.loop(0, groups)
            def _(k):
                stage[half, :, span(k, group_wide)] = inbox[k, rows, pl.ds(0, group_wide)].astype(f32)

        @pl.when(sec < last)
        def _():
            def decode(k, acc):
                cols = span(k, group_wide)
                send(c, slot, k).wait_recv()
                scales = inbox[k, rows, pl.ds(group_wide, LANES)].astype(f32)
                scale = jnp.concatenate([scales[:, j:j + 1] for j in range(GROUP)], axis=0)
                value = dot(stack(inbox[k, rows, pl.ds(0, group_wide)]), matrix[...]) * scale
                value = unstack(value, CHUNK) * signs[1:2, cols]
                low = value.astype(bf16)
                stage[half, :, cols] = value
                inbox[k, rows, pl.ds(0, group_wide)] = low
                return acc + dot(low, weight[cols, :])

            grad_act[rows, :] = lax.fori_loop(0, groups, decode, jnp.zeros((CHUNK, rank), f32))

        pre_here = pre[rows, :]
        sigma = jax.nn.sigmoid(pre_here)
        grad_pre = (grad_act[rows, :] * sigma * (1.0 + pre_here * (1.0 - sigma))).astype(bf16)
        right[rows, :] = grad_pre
        right[span(c + chunks, CHUNK), :] = (pre_here * sigma).astype(bf16)
        inner = jnp.sum(grad_pre.astype(f32) * pre_here, axis=-1, keepdims=True) / width
        scale_inv = sinv[rows, 0:1]

        def layer_block(cols):
            grad_hidden = dot(grad_pre, weight[cols, :], 1, 1)
            normed = x[rows, cols].astype(f32) * scale_inv
            term = grad_hidden * normed
            total = term[0:8]
            for j in range(1, CHUNK // 8):
                total = total + term[8 * j:8 * j + 8]
            grad_out = stage[half, :, cols] + scale_inv * (grad_hidden * gain[:, cols] - normed * inner)
            return total, grad_out

        @pl.when(sec == 0)
        def _():
            @pl.loop(0, groups)
            def _(k):
                cols = span(k, group_wide)
                total, grad_out = layer_block(cols)
                gacc[:, cols] += total
                stage[half, :, cols] = grad_out

        @pl.when(sec > 0)
        def _():
            @pl.when(c >= SLOTS)
            def _():
                for k in range(groups):
                    send(c - SLOTS, slot, k).wait_send()

            @pl.loop(0, groups)
            def _(k):
                cols = span(k, group_wide)
                total, grad_out = layer_block(cols)
                value = grad_out + fb[kept, cols]
                sign = signs[0:1, cols]
                turned = stack(value * sign)
                high = turned.astype(bf16)
                low = (turned - high.astype(f32)).astype(bf16)
                rotated = dot(jnp.concatenate([high, low], axis=0), matrix[...])
                rotated = rotated[:GROUP * CHUNK] + rotated[GROUP * CHUNK:]
                scale = jnp.sum(jnp.abs(rotated), axis=-1, keepdims=True) / HB + eps_scale
                scale = scale.astype(bf16).astype(f32)
                levels = jnp.clip(rotated * (1.0 / scale), -1.0, 1.0).astype(bf16)
                decoded = unstack(dot(levels, matrix[...]) * scale, CHUNK) * sign
                gacc[:, cols] += total
                stage[half, :, cols] = grad_out
                outbox[slot, k, :, pl.ds(0, group_wide)] = unstack(levels, CHUNK)
                scales = jnp.zeros((CHUNK, LANES), f32)
                for j in range(GROUP):
                    scales = jnp.where(lane == j, scale[j * CHUNK:(j + 1) * CHUNK], scales)
                outbox[slot, k, :, pl.ds(group_wide, LANES)] = scales.astype(bf16)
                send(c, slot, k).start()
                fb[kept, cols] = value - decoded

        store(c, half).start()

    gsum[...] = jnp.sum(gacc[...], axis=0, keepdims=True)

    def sum_copy(k):
        target = lax.rem(here + k, peers)
        return pltpu.make_async_remote_copy(
            src_ref=gsum.at[:, span(target, shard)],
            dst_ref=gparts.at[k],
            send_sem=s_send.at[k],
            recv_sem=s_recv.at[k],
            device_id={"fsdp": target},
            device_id_type=MESH,
        )

    for k in range(1, peers):
        sum_copy(k).start()

    piece = 256

    def share(owner, into, spot):
        @pl.loop(0, shard // piece)
        def _(k):
            cols = pl.ds(pl.multiple_of(owner * shard + k * piece, piece), piece)
            first = owner * shard + k * piece
            part = pl.ds(pl.multiple_of(lax.rem(first, group_wide), piece), piece)
            left = jnp.concatenate([hidden[:, cols], inbox[first // group_wide, :, part]], axis=0)
            into[spot, span(k, piece), :] = dot(left, right[...], 0, 0).astype(bf16)

    def sibling_copy(spot):
        return pltpu.make_async_remote_copy(
            src_ref=sib_out.at[spot],
            dst_ref=sib_in.at[spot],
            send_sem=b_send.at[spot],
            recv_sem=b_recv.at[spot],
            device_id={"fsdp": sibling},
            device_id_type=MESH,
        )

    def chain_copy(spot, way):
        arrive = spot
        target = here + 2
        if way == 1:
            target = here - 2
            arrive = spot + (chips - spot) * (chip - 1 == spot).astype(jnp.int32)
        return pltpu.make_async_remote_copy(
            src_ref=own_part.at[spot],
            dst_ref=chain_in.at[arrive],
            send_sem=c_send.at[spot],
            recv_sem=c_recv.at[arrive],
            device_id={"fsdp": target},
            device_id_type=MESH,
        )

    def arrived(slot):
        pltpu.make_async_remote_copy(
            src_ref=own_part.at[0],
            dst_ref=chain_in.at[slot],
            send_sem=c_send.at[0],
            recv_sem=c_recv.at[slot],
            device_id={"fsdp": sibling},
            device_id_type=MESH,
        ).wait_recv()

    def merge(spot, inner_chip):
        sibling_copy(spot).wait_recv()

        @pl.when(inner_chip)
        def _():
            arrived(spot)

            @pl.loop(0, shard // piece)
            def _(k):
                part = span(k, piece)
                own_part[spot, part, :] = (
                    own_part[spot, part, :].astype(f32) + sib_in[spot, part, :].astype(f32)
                    + chain_in[spot, part, :].astype(f32)
                ).astype(bf16)

        @pl.when(jnp.logical_not(inner_chip))
        def _():
            @pl.loop(0, shard // piece)
            def _(k):
                part = span(k, piece)
                own_part[spot, part, :] = (
                    own_part[spot, part, :].astype(f32) + sib_in[spot, part, :].astype(f32)
                ).astype(bf16)

    def go_right(k):
        spot = chips - 1 - k

        @pl.when(spot > chip)
        def _():
            merge(spot, chip > 0)
            chain_copy(spot, 0).start()

    def go_left(k):
        @pl.when(k < chip)
        def _():
            merge(k, chip < chips - 1)
            chain_copy(k, 1).start()

    @pl.loop(0, chips)
    def _(k):
        low_half = (chip < chips // 2).astype(jnp.int32)
        spot = low_half * (chips - 1 - k) + (1 - low_half) * k
        share(spot * 2 + 1 - core, sib_out, spot)
        sibling_copy(spot).start()
        share(spot * 2 + core, own_part, spot)

        @pl.when(jnp.logical_and(chip == 0, k > 0))
        def _():
            go_right(k - 1)

        @pl.when(jnp.logical_and(chip == chips - 1, k > 0))
        def _():
            go_left(k - 1)

    @pl.loop(0, chips)
    def _(k):
        @pl.when(jnp.logical_and(chip > 0, chip < chips // 2))
        def _():
            go_right(k)
            go_left(k)

        @pl.when(jnp.logical_and(chip >= chips // 2, chip < chips - 1))
        def _():
            go_left(k)
            go_right(k)

    sibling_copy(chip).wait_recv()

    @pl.loop(0, shard // piece)
    def _(k):
        part = span(k, piece)
        dw[part, :] = own_part[chip, part, :].astype(f32) + sib_in[chip, part, :].astype(f32)

    def add_arrived(slot):
        arrived(slot)

        @pl.loop(0, shard // piece)
        def _(k):
            part = span(k, piece)
            dw[part, :] += chain_in[slot, part, :].astype(f32)

    @pl.when(chip > 0)
    def _():
        add_arrived(chip)

    @pl.when(chip < chips - 1)
    def _():
        add_arrived(chips)

    total = gsum[:, span(here, shard)]
    for k in range(1, peers):
        sum_copy(k).wait_recv()
        total = total + gparts[k]
    gain_out[...] = total

    for c in range(max(0, chunks - 2), chunks):
        store(c, c % 2).wait()

    @pl.when(sec > 0)
    def _():
        for c in range(max(0, chunks - SLOTS), chunks):
            for k in range(groups):
                send(c, c % SLOTS, k).wait_send()

    for k in range(1, peers):
        gain_copy(k).wait_send()
        sum_copy(k).wait_send()
    pass_right(here, finish)
    pass_left(here, finish)
    pass_sibling(here, finish)
    for distance in range(1, chips):
        @pl.when(chip >= distance)
        def _():
            pass_right(here - 2 * distance, finish)
            pass_sibling(here - 2 * distance, finish)

        @pl.when(chip + distance < chips)
        def _():
            pass_left(here + 2 * distance, finish)
            pass_sibling(here + 2 * distance, finish)

    @pl.loop(0, chips)
    def _(k):
        sibling_copy(k).wait_send()

        @pl.when(k > chip)
        def _():
            chain_copy(k, 0).wait_send()

        @pl.when(k < chip)
        def _():
            chain_copy(k, 1).wait_send()


def reorder_kernel(order, *refs):
    count = len(refs) // 2
    for source, target in zip(refs[:count], refs[count:]):
        target[...] = source[...]


def reorder(order, arrays, scatter):
    micro_count, token_count, width = arrays[0].shape
    rows = 32
    straight = pl.BlockSpec((1, rows, width), lambda m, i, order: (m, i, 0))
    picked = pl.BlockSpec((1, rows, width), lambda m, i, order: (order[m], i, 0))
    source, target = (straight, picked) if scatter else (picked, straight)
    return pl.pallas_call(
        reorder_kernel,
        out_shape=tuple(jax.ShapeDtypeStruct(a.shape, a.dtype) for a in arrays),
        grid_spec=pltpu.PrefetchScalarGridSpec(
            num_scalar_prefetch=1,
            grid=(micro_count, token_count // rows),
            in_specs=[source] * len(arrays),
            out_specs=(target,) * len(arrays),
        ),
    )(order, *arrays)


def per_device(
    section_inputs, top_grads, weights, norm_gains, feedback, rotation_bits, batch_order
):
    section_count = lax.axis_size("section")
    peers = lax.axis_size("fsdp")
    section_here = lax.axis_index("section")
    micro_count, token_count, width = section_inputs.shape[1:]
    shard, rank = weights.shape[1:]
    rows = micro_count * token_count
    chunks = rows // CHUNK
    chips = peers // 2
    groups = width // (GROUP * HB)
    above = jnp.minimum(section_here + 1, section_count - 1)
    bits = jnp.stack([rotation_bits[section_here], rotation_bits[above]])
    signs = (1 - 2 * bits).astype(f32)
    x, top = reorder(batch_order, (section_inputs[0], top_grads), False)
    vmem = pl.BlockSpec(memory_space=pltpu.VMEM)
    hbm = pl.BlockSpec(memory_space=pl.ANY)
    dma = pltpu.SemaphoreType.DMA
    gout, dw, gain_share, fb_out = pl.pallas_call(
        functools.partial(relay_kernel, section_count, peers),
        out_shape=(
            jax.ShapeDtypeStruct((rows, width), f32),
            jax.ShapeDtypeStruct((shard, rank), f32),
            jax.ShapeDtypeStruct((1, shard), f32),
            jax.ShapeDtypeStruct((token_count, width), f32),
        ),
        in_specs=[vmem, hbm, hbm, vmem, vmem, vmem, hbm],
        out_specs=(hbm, vmem, vmem, vmem),
        scratch_shapes=[
            pltpu.VMEM((width, rank), bf16),
            pltpu.VMEM((1, width), f32),
            pltpu.VMEM((groups, rows, GROUP * HB + LANES), bf16),
            pltpu.VMEM((SLOTS, groups, CHUNK, GROUP * HB + LANES), bf16),
            pltpu.VMEM((rows, width), bf16),
            pltpu.VMEM((2, CHUNK, width), f32),
            pltpu.VMEM((rows, rank), f32),
            pltpu.VMEM((rows, rank), f32),
            pltpu.VMEM((2 * rows, rank), bf16),
            pltpu.VMEM((rows, LANES), f32),
            pltpu.VMEM((8, width), f32),
            pltpu.VMEM((1, width), f32),
            pltpu.VMEM((peers, 1, shard), f32),
            pltpu.VMEM((chips, shard, rank), bf16),
            pltpu.VMEM((chips, shard, rank), bf16),
            pltpu.VMEM((chips, shard, rank), bf16),
            pltpu.VMEM((chips + 1, shard, rank), bf16),
            dma((chunks, groups)), dma((SLOTS, groups)), dma((2,)), dma, dma((groups,)), dma,
            dma((peers,)), dma((3 * chips,)),
            dma((peers,)), dma((peers,)),
            dma((peers,)), dma((peers,)),
            dma((chips,)), dma((chips,)),
            dma((chips + 1,)), dma((chips,)),
        ],
        compiler_params=pltpu.CompilerParams(
            collective_id=0, has_side_effects=True, vmem_limit_bytes=60 * 1024 * 1024
        ),
    )(
        x.reshape(rows, width), top.reshape(rows, width), weights[0], norm_gains, signs,
        hadamard(HB).astype(bf16), feedback[0],
    )
    (input_grads,) = reorder(batch_order, (gout.reshape(micro_count, token_count, width),), True)
    return (input_grads[None], dw[None], gain_share, fb_out[None])


def solution(mesh):
    return jax.shard_map(
        per_device,
        mesh=mesh,
        in_specs=(
            P("section", None, "fsdp", None),
            P(None, "fsdp", None),
            P("section", "fsdp", None),
            P("section", "fsdp"),
            P("section", "fsdp", None),
            P(),
            P(),
        ),
        out_specs=(
            P("section", None, "fsdp", None),
            P("section", "fsdp", None),
            P("section", "fsdp"),
            P("section", "fsdp", None),
        ),
        check_vma=False,
    )
```

```python
import functools

import jax
import jax.numpy as jnp
from jax import lax
from jax.experimental import pallas as pl
from jax.experimental.pallas import tpu as pltpu
from jax.sharding import PartitionSpec as P

HB = 256
CHUNK = 32
SLOTS = 4
LANES = 128
GROUP = 8
MESH = pl.DeviceIdType.MESH

eps_norm = 1e-05
eps_scale = 1e-06
f32 = jnp.float32
bf16 = jnp.bfloat16


def hadamard(order_size):
    position = jnp.arange(order_size, dtype=jnp.int32)
    shared_bits = jnp.bitwise_and(position[:, None], position[None, :])
    parity = jnp.zeros((order_size, order_size), jnp.int32)
    for bit_place in range(order_size.bit_length() - 1):
        parity = parity + jnp.bitwise_and(jnp.right_shift(shared_bits, bit_place), 1)
    return (1 - 2 * (parity % 2)).astype(f32) / jnp.sqrt(f32(order_size))


def dot(a, b, ca=1, cb=0):
    return lax.dot_general(a, b, (((ca,), (cb,)), ((), ())), preferred_element_type=f32)


def stack(value):
    return jnp.concatenate(
        [value[:, j * HB:(j + 1) * HB] for j in range(value.shape[1] // HB)], axis=0
    )


def unstack(value, rows):
    return jnp.concatenate(
        [value[j * rows:(j + 1) * rows] for j in range(value.shape[0] // rows)], axis=1
    )


def span(index, size):
    return pl.ds(pl.multiple_of(index * size, size), size)


def relay_kernel(
    sections, peers, x_in, top, weight_in, gain_in, signs, matrix, fb_in, flag,
    gout, dw, gain_out, fb,
    x, weight, gain, inbox, outbox, hidden, stage, pre, grad_act, right, sinv, gacc,
    gsum, gparts, own_part, sib_out, sib_in, chain_in,
    recv_sem, send_sem, out_sem, fb_sem, top_sem, own_sem, x_sem,
    w_recv, w_send, g_recv, g_send, s_recv, s_send, b_recv, b_send, c_recv, c_send,
):
    sec = lax.axis_index("section")
    here = lax.axis_index("fsdp")
    chips = peers // 2
    chip = here // 2
    core = lax.rem(here, 2)
    sibling = here + 1 - 2 * core
    rows_all, width = x.shape
    rank = weight.shape[1]
    shard = width // peers
    held = fb.shape[0]
    chunks = rows_all // CHUNK
    last = sections - 1
    wide = 1024
    barrier = pltpu.get_barrier_semaphore()

    for k in range(1, peers):
        pl.semaphore_signal(
            barrier, inc=1, device_id={"fsdp": lax.rem(here + k, peers)}, device_id_type=MESH
        )

    @pl.when(sec < last)
    def _():
        pl.semaphore_signal(barrier, inc=1, device_id={"section": sec + 1}, device_id_type=MESH)

    own_copy = pltpu.make_async_copy(weight_in, weight.at[span(here, shard)], own_sem)
    own_copy.start()
    x_copy = pltpu.make_async_copy(x_in, x, x_sem)
    x_copy.start()
    fb_copy = pltpu.make_async_copy(fb_in, fb, fb_sem)
    fb_copy.start()
    group_wide = GROUP * HB
    groups = width // group_wide
    top_copies = [
        pltpu.make_async_copy(
            top.at[:, pl.ds(k * group_wide, group_wide)],
            inbox.at[k, :, pl.ds(0, group_wide)],
            top_sem.at[k],
        )
        for k in range(groups)
    ]

    @pl.when(sec == last)
    def _():
        for copy in top_copies:
            copy.start()

    gain[:, span(here, shard)] = gain_in[...]
    gacc[...] = jnp.zeros_like(gacc)
    pre[...] = jnp.zeros_like(pre)
    grad_act[...] = jnp.zeros_like(grad_act)
    pl.semaphore_wait(barrier, peers - 1 + (sec > 0).astype(jnp.int32))

    own_copy.wait()

    def weight_copy(owner, target, way):
        return pltpu.make_async_remote_copy(
            src_ref=weight.at[span(owner, shard)],
            dst_ref=weight.at[span(owner, shard)],
            send_sem=w_send.at[way * chips + owner // 2],
            recv_sem=w_recv.at[owner],
            device_id={"fsdp": target},
            device_id_type=MESH,
        )

    def pass_right(owner, act):
        @pl.when(chip < chips - 1)
        def _():
            act(weight_copy(owner, here + 2, 0))

    def pass_left(owner, act):
        @pl.when(chip > 0)
        def _():
            act(weight_copy(owner, here - 2, 1))

    def pass_sibling(owner, act):
        act(weight_copy(owner, sibling, 2))

    def start(copy):
        copy.start()

    def finish(copy):
        copy.wait_send()

    def gain_copy(k):
        return pltpu.make_async_remote_copy(
            src_ref=gain.at[:, span(here, shard)],
            dst_ref=gain.at[:, span(here, shard)],
            send_sem=g_send.at[k],
            recv_sem=g_recv.at[k],
            device_id={"fsdp": lax.rem(here + k, peers)},
            device_id_type=MESH,
        )

    for k in range(1, peers):
        gain_copy(k).start()
    pass_right(here, start)
    pass_left(here, start)
    pass_sibling(here, start)

    swapped = jnp.broadcast_to(flag[0:1, 0:1], (CHUNK, wide)) == 1

    def exchange(ref, c, cols):
        here_rows, there_rows = span(c, CHUNK), span(c + chunks // 2, CHUNK)
        first = ref[here_rows, cols].astype(f32)
        second = ref[there_rows, cols].astype(f32)
        ref[here_rows, cols] = jnp.where(swapped, second, first).astype(bf16)
        ref[there_rows, cols] = jnp.where(swapped, first, second).astype(bf16)

    x_copy.wait()

    @pl.loop(0, chunks // 2)
    def _(c):
        @pl.loop(0, width // wide)
        def _(k):
            exchange(x, c, span(k, wide))

    @pl.loop(0, chunks)
    def _(c):
        rows = span(c, CHUNK)

        def square(k, acc):
            part = x[rows, span(k, wide)].astype(f32)
            part = part * part
            for j in range(wide // LANES):
                acc = acc + part[:, j * LANES:(j + 1) * LANES]
            return acc

        acc = lax.fori_loop(0, width // wide, square, jnp.zeros((CHUNK, LANES), f32))
        scale_inv = lax.rsqrt(jnp.sum(acc, axis=-1, keepdims=True) / width + eps_norm)
        sinv[rows, :] = jnp.broadcast_to(scale_inv, (CHUNK, LANES))

    for k in range(1, peers):
        pltpu.make_async_remote_copy(
            src_ref=gain.at[:, span(here, shard)],
            dst_ref=gain.at[:, span(lax.rem(here + peers - k, peers), shard)],
            send_sem=g_send.at[k],
            recv_sem=g_recv.at[k],
            device_id={"fsdp": lax.rem(here + k, peers)},
            device_id_type=MESH,
        ).wait_recv()

    @pl.loop(0, chunks)
    def _(c):
        rows = span(c, CHUNK)
        scale_inv = sinv[rows, 0:1]

        @pl.loop(0, width // wide)
        def _(k):
            cols = span(k, wide)
            hidden[rows, cols] = (x[rows, cols].astype(f32) * scale_inv * gain[:, cols]).astype(bf16)

    @pl.when(sec == last)
    def _():
        for copy in top_copies:
            copy.wait()

        @pl.loop(0, chunks // 2)
        def _(c):
            @pl.loop(0, groups)
            def _(k):
                for j in range(group_wide // wide):
                    exchange(inbox.at[k], c, pl.ds(j * wide, wide))

    def accumulate(spot):
        other = spot * 2 + 1 - core
        weight_copy(other, sibling, 2).wait_recv()
        for owner in (spot * 2 + core, other):
            cols = span(owner, shard)
            pre[...] += dot(hidden[:, cols], weight[cols, :])

            @pl.when(sec == last)
            def _():
                first = owner * shard
                part = pl.ds(pl.multiple_of(lax.rem(first, group_wide), shard), shard)
                grad_act[...] += dot(inbox[first // group_wide, :, part], weight[cols, :])

    def accumulate_around(distance):
        @pl.when(chip >= distance)
        def _():
            accumulate(chip - distance)

        if distance > 0:
            @pl.when(chip + distance < chips)
            def _():
                accumulate(chip + distance)

    for distance in range(1, chips):
        @pl.when(chip >= distance)
        def _():
            owner = here - 2 * distance
            weight_copy(owner, sibling, 2).wait_recv()
            pass_right(owner, start)
            pass_sibling(owner, start)

        @pl.when(chip + distance < chips)
        def _():
            owner = here + 2 * distance
            weight_copy(owner, sibling, 2).wait_recv()
            pass_left(owner, start)
            pass_sibling(owner, start)

        accumulate_around(distance - 1)
    accumulate_around(chips - 1)

    fb_copy.wait()
    lane = lax.broadcasted_iota(jnp.int32, (CHUNK, LANES), 1)

    def send(c, slot, k):
        return pltpu.make_async_remote_copy(
            src_ref=outbox.at[slot, k],
            dst_ref=inbox.at[k, span(c, CHUNK)],
            send_sem=send_sem.at[slot, k],
            recv_sem=recv_sem.at[c, k],
            device_id={"section": sec - 1},
            device_id_type=MESH,
        )

    def store(c, half):
        return pltpu.make_async_copy(stage.at[half], gout.at[span(c, CHUNK)], out_sem.at[half])

    @pl.loop(0, chunks)
    def _(c):
        rows = span(c, CHUNK)
        kept = span(lax.rem(c, held // CHUNK), CHUNK)
        half = lax.rem(c, 2)
        slot = lax.rem(c, SLOTS)

        @pl.when(c >= 2)
        def _():
            store(c - 2, half).wait()

        @pl.when(sec == last)
        def _():
            @pl.loop(0, groups)
            def _(k):
                stage[half, :, span(k, group_wide)] = inbox[k, rows, pl.ds(0, group_wide)].astype(f32)

        @pl.when(sec < last)
        def _():
            acc = jnp.zeros((CHUNK, rank), f32)
            held_low = None
            for k in range(groups):
                cols = pl.ds(k * group_wide, group_wide)
                send(c, slot, k).wait_recv()
                scales = inbox[k, rows, pl.ds(group_wide, LANES)].astype(f32)
                scale = jnp.concatenate([scales[:, j:j + 1] for j in range(GROUP)], axis=0)
                value = dot(stack(inbox[k, rows, pl.ds(0, group_wide)]), matrix[...]) * scale
                if k > 0:
                    acc = acc + dot(held_low, weight[pl.ds((k - 1) * group_wide, group_wide), :])
                value = unstack(value, CHUNK) * signs[1:2, cols]
                held_low = value.astype(bf16)
                stage[half, :, cols] = value
                inbox[k, rows, pl.ds(0, group_wide)] = held_low
            acc = acc + dot(held_low, weight[pl.ds((groups - 1) * group_wide, group_wide), :])
            grad_act[rows, :] = acc

        pre_here = pre[rows, :]
        sigma = jax.nn.sigmoid(pre_here)
        grad_pre = (grad_act[rows, :] * sigma * (1.0 + pre_here * (1.0 - sigma))).astype(bf16)
        right[rows, :] = grad_pre
        right[span(c + chunks, CHUNK), :] = (pre_here * sigma).astype(bf16)
        inner = jnp.sum(grad_pre.astype(f32) * pre_here, axis=-1, keepdims=True) / width
        scale_inv = sinv[rows, 0:1]

        def back(k):
            return dot(grad_pre, weight[pl.ds(k * group_wide, group_wide), :], 1, 1)

        def layer_block(cols, grad_hidden):
            normed = x[rows, cols].astype(f32) * scale_inv
            term = grad_hidden * normed
            total = term[0:8]
            for j in range(1, CHUNK // 8):
                total = total + term[8 * j:8 * j + 8]
            grad_out = stage[half, :, cols] + scale_inv * (grad_hidden * gain[:, cols] - normed * inner)
            return total, grad_out

        @pl.when(sec == 0)
        def _():
            for k in range(groups):
                cols = pl.ds(k * group_wide, group_wide)
                total, grad_out = layer_block(cols, back(k))
                gacc[:, cols] += total
                stage[half, :, cols] = grad_out

        @pl.when(sec > 0)
        def _():
            @pl.when(c >= SLOTS)
            def _():
                for k in range(groups):
                    send(c - SLOTS, slot, k).wait_send()

            following = back(0)
            for k in range(groups):
                cols = pl.ds(k * group_wide, group_wide)
                total, grad_out = layer_block(cols, following)
                if k + 1 < groups:
                    following = back(k + 1)
                value = grad_out + fb[kept, cols]
                sign = signs[0:1, cols]
                turned = stack(value * sign)
                high = turned.astype(bf16)
                low = (turned - high.astype(f32)).astype(bf16)
                rotated = dot(jnp.concatenate([high, low], axis=0), matrix[...])
                rotated = rotated[:GROUP * CHUNK] + rotated[GROUP * CHUNK:]
                scale = jnp.sum(jnp.abs(rotated), axis=-1, keepdims=True) / HB + eps_scale
                scale = scale.astype(bf16).astype(f32)
                levels = jnp.clip(rotated * (1.0 / scale), -1.0, 1.0).astype(bf16)
                decoded = unstack(dot(levels, matrix[...]) * scale, CHUNK) * sign
                gacc[:, cols] += total
                stage[half, :, cols] = grad_out
                outbox[slot, k, :, pl.ds(0, group_wide)] = unstack(levels, CHUNK)
                scales = jnp.zeros((CHUNK, LANES), f32)
                for j in range(GROUP):
                    scales = jnp.where(lane == j, scale[j * CHUNK:(j + 1) * CHUNK], scales)
                outbox[slot, k, :, pl.ds(group_wide, LANES)] = scales.astype(bf16)
                send(c, slot, k).start()
                fb[kept, cols] = value - decoded

        store(c, half).start()

    gsum[...] = jnp.sum(gacc[...], axis=0, keepdims=True)

    def sum_copy(k):
        target = lax.rem(here + k, peers)
        return pltpu.make_async_remote_copy(
            src_ref=gsum.at[:, span(target, shard)],
            dst_ref=gparts.at[k],
            send_sem=s_send.at[k],
            recv_sem=s_recv.at[k],
            device_id={"fsdp": target},
            device_id_type=MESH,
        )

    for k in range(1, peers):
        sum_copy(k).start()

    piece = 256

    def share(owner, into, spot):
        @pl.loop(0, shard // piece)
        def _(k):
            cols = pl.ds(pl.multiple_of(owner * shard + k * piece, piece), piece)
            first = owner * shard + k * piece
            part = pl.ds(pl.multiple_of(lax.rem(first, group_wide), piece), piece)
            left = jnp.concatenate([hidden[:, cols], inbox[first // group_wide, :, part]], axis=0)
            into[spot, span(k, piece), :] = dot(left, right[...], 0, 0).astype(bf16)

    def sibling_copy(spot):
        return pltpu.make_async_remote_copy(
            src_ref=sib_out.at[spot],
            dst_ref=sib_in.at[spot],
            send_sem=b_send.at[spot],
            recv_sem=b_recv.at[spot],
            device_id={"fsdp": sibling},
            device_id_type=MESH,
        )

    def chain_copy(spot, way):
        arrive = spot
        target = here + 2
        if way == 1:
            target = here - 2
            arrive = spot + (chips - spot) * (chip - 1 == spot).astype(jnp.int32)
        return pltpu.make_async_remote_copy(
            src_ref=own_part.at[spot],
            dst_ref=chain_in.at[arrive],
            send_sem=c_send.at[spot],
            recv_sem=c_recv.at[arrive],
            device_id={"fsdp": target},
            device_id_type=MESH,
        )

    def arrived(slot):
        pltpu.make_async_remote_copy(
            src_ref=own_part.at[0],
            dst_ref=chain_in.at[slot],
            send_sem=c_send.at[0],
            recv_sem=c_recv.at[slot],
            device_id={"fsdp": sibling},
            device_id_type=MESH,
        ).wait_recv()

    def merge(spot, inner_chip):
        sibling_copy(spot).wait_recv()

        @pl.when(inner_chip)
        def _():
            arrived(spot)

            @pl.loop(0, shard // piece)
            def _(k):
                part = span(k, piece)
                own_part[spot, part, :] = (
                    own_part[spot, part, :].astype(f32) + sib_in[spot, part, :].astype(f32)
                    + chain_in[spot, part, :].astype(f32)
                ).astype(bf16)

        @pl.when(jnp.logical_not(inner_chip))
        def _():
            @pl.loop(0, shard // piece)
            def _(k):
                part = span(k, piece)
                own_part[spot, part, :] = (
                    own_part[spot, part, :].astype(f32) + sib_in[spot, part, :].astype(f32)
                ).astype(bf16)

    def go_right(k):
        spot = chips - 1 - k

        @pl.when(spot > chip)
        def _():
            merge(spot, chip > 0)
            chain_copy(spot, 0).start()

    def go_left(k):
        @pl.when(k < chip)
        def _():
            merge(k, chip < chips - 1)
            chain_copy(k, 1).start()

    @pl.loop(0, chips)
    def _(k):
        low_half = (chip < chips // 2).astype(jnp.int32)
        spot = low_half * (chips - 1 - k) + (1 - low_half) * k
        share(spot * 2 + 1 - core, sib_out, spot)
        sibling_copy(spot).start()
        share(spot * 2 + core, own_part, spot)

        @pl.when(jnp.logical_and(chip == 0, k > 0))
        def _():
            go_right(k - 1)

        @pl.when(jnp.logical_and(chip == chips - 1, k > 0))
        def _():
            go_left(k - 1)

    @pl.loop(0, chips)
    def _(k):
        @pl.when(jnp.logical_and(chip > 0, chip < chips // 2))
        def _():
            go_right(k)
            go_left(k)

        @pl.when(jnp.logical_and(chip >= chips // 2, chip < chips - 1))
        def _():
            go_left(k)
            go_right(k)

    sibling_copy(chip).wait_recv()

    @pl.loop(0, shard // piece)
    def _(k):
        part = span(k, piece)
        dw[part, :] = own_part[chip, part, :].astype(f32) + sib_in[chip, part, :].astype(f32)

    def add_arrived(slot):
        arrived(slot)

        @pl.loop(0, shard // piece)
        def _(k):
            part = span(k, piece)
            dw[part, :] += chain_in[slot, part, :].astype(f32)

    @pl.when(chip > 0)
    def _():
        add_arrived(chip)

    @pl.when(chip < chips - 1)
    def _():
        add_arrived(chips)

    total = gsum[:, span(here, shard)]
    for k in range(1, peers):
        sum_copy(k).wait_recv()
        total = total + gparts[k]
    gain_out[...] = total

    for c in range(max(0, chunks - 2), chunks):
        store(c, c % 2).wait()

    @pl.when(sec > 0)
    def _():
        for c in range(max(0, chunks - SLOTS), chunks):
            for k in range(groups):
                send(c, c % SLOTS, k).wait_send()

    for k in range(1, peers):
        gain_copy(k).wait_send()
        sum_copy(k).wait_send()
    pass_right(here, finish)
    pass_left(here, finish)
    pass_sibling(here, finish)
    for distance in range(1, chips):
        @pl.when(chip >= distance)
        def _():
            pass_right(here - 2 * distance, finish)
            pass_sibling(here - 2 * distance, finish)

        @pl.when(chip + distance < chips)
        def _():
            pass_left(here + 2 * distance, finish)
            pass_sibling(here + 2 * distance, finish)

    @pl.loop(0, chips)
    def _(k):
        sibling_copy(k).wait_send()

        @pl.when(k > chip)
        def _():
            chain_copy(k, 0).wait_send()

        @pl.when(k < chip)
        def _():
            chain_copy(k, 1).wait_send()


def reorder_kernel(order, source, target):
    target[...] = source[...]


def reorder(order, array):
    micro_count, token_count, width = array.shape
    rows = 16
    return pl.pallas_call(
        reorder_kernel,
        out_shape=jax.ShapeDtypeStruct(array.shape, array.dtype),
        grid_spec=pltpu.PrefetchScalarGridSpec(
            num_scalar_prefetch=1,
            grid=(micro_count, token_count // rows),
            in_specs=[pl.BlockSpec((1, rows, width), lambda m, i, order: (m, i, 0))],
            out_specs=pl.BlockSpec((1, rows, width), lambda m, i, order: (order[m], i, 0)),
        ),
    )(order, array)


def per_device(
    section_inputs, top_grads, weights, norm_gains, feedback, rotation_bits, batch_order
):
    section_count = lax.axis_size("section")
    peers = lax.axis_size("fsdp")
    section_here = lax.axis_index("section")
    micro_count, token_count, width = section_inputs.shape[1:]
    shard, rank = weights.shape[1:]
    rows = micro_count * token_count
    chunks = rows // CHUNK
    chips = peers // 2
    groups = width // (GROUP * HB)
    above = jnp.minimum(section_here + 1, section_count - 1)
    bits = jnp.stack([rotation_bits[section_here], rotation_bits[above]])
    signs = (1 - 2 * bits).astype(f32)
    assert micro_count == 2
    flag = jnp.broadcast_to(batch_order[0], (1, LANES))
    vmem = pl.BlockSpec(memory_space=pltpu.VMEM)
    hbm = pl.BlockSpec(memory_space=pl.ANY)
    dma = pltpu.SemaphoreType.DMA
    gout, dw, gain_share, fb_out = pl.pallas_call(
        functools.partial(relay_kernel, section_count, peers),
        out_shape=(
            jax.ShapeDtypeStruct((rows, width), f32),
            jax.ShapeDtypeStruct((shard, rank), f32),
            jax.ShapeDtypeStruct((1, shard), f32),
            jax.ShapeDtypeStruct((token_count, width), f32),
        ),
        in_specs=[hbm, hbm, hbm, vmem, vmem, vmem, hbm, vmem],
        out_specs=(hbm, vmem, vmem, vmem),
        scratch_shapes=[
            pltpu.VMEM((rows, width), bf16),
            pltpu.VMEM((width, rank), bf16),
            pltpu.VMEM((1, width), f32),
            pltpu.VMEM((groups, rows, GROUP * HB + LANES), bf16),
            pltpu.VMEM((SLOTS, groups, CHUNK, GROUP * HB + LANES), bf16),
            pltpu.VMEM((rows, width), bf16),
            pltpu.VMEM((2, CHUNK, width), f32),
            pltpu.VMEM((rows, rank), f32),
            pltpu.VMEM((rows, rank), f32),
            pltpu.VMEM((2 * rows, rank), bf16),
            pltpu.VMEM((rows, LANES), f32),
            pltpu.VMEM((8, width), f32),
            pltpu.VMEM((1, width), f32),
            pltpu.VMEM((peers, 1, shard), f32),
            pltpu.VMEM((chips, shard, rank), bf16),
            pltpu.VMEM((chips, shard, rank), bf16),
            pltpu.VMEM((chips, shard, rank), bf16),
            pltpu.VMEM((chips + 1, shard, rank), bf16),
            dma((chunks, groups)), dma((SLOTS, groups)), dma((2,)), dma, dma((groups,)), dma, dma,
            dma((peers,)), dma((3 * chips,)),
            dma((peers,)), dma((peers,)),
            dma((peers,)), dma((peers,)),
            dma((chips,)), dma((chips,)),
            dma((chips + 1,)), dma((chips,)),
        ],
        compiler_params=pltpu.CompilerParams(
            collective_id=0, has_side_effects=True, vmem_limit_bytes=60 * 1024 * 1024
        ),
    )(
        section_inputs.reshape(rows, width), top_grads.reshape(rows, width), weights[0],
        norm_gains, signs, hadamard(HB).astype(bf16), feedback[0], flag,
    )
    input_grads = reorder(batch_order, gout.reshape(micro_count, token_count, width))
    return (input_grads[None], dw[None], gain_share, fb_out[None])


def solution(mesh):
    return jax.shard_map(
        per_device,
        mesh=mesh,
        in_specs=(
            P("section", None, "fsdp", None),
            P(None, "fsdp", None),
            P("section", "fsdp", None),
            P("section", "fsdp"),
            P("section", "fsdp", None),
            P(),
            P(),
        ),
        out_specs=(
            P("section", None, "fsdp", None),
            P("section", "fsdp", None),
            P("section", "fsdp"),
            P("section", "fsdp", None),
        ),
        check_vma=False,
    )
```

```python
import functools

import jax
import jax.numpy as jnp
from jax import lax
from jax.experimental import pallas as pl
from jax.experimental.pallas import tpu as pltpu
from jax.sharding import PartitionSpec as P

HB = 256
CHUNK = 32
SLOTS = 4
LANES = 128
GROUP = 8
MESH = pl.DeviceIdType.MESH

eps_norm = 1e-05
eps_scale = 1e-06
f32 = jnp.float32
bf16 = jnp.bfloat16


def hadamard(order_size):
    position = jnp.arange(order_size, dtype=jnp.int32)
    shared_bits = jnp.bitwise_and(position[:, None], position[None, :])
    parity = jnp.zeros((order_size, order_size), jnp.int32)
    for bit_place in range(order_size.bit_length() - 1):
        parity = parity + jnp.bitwise_and(jnp.right_shift(shared_bits, bit_place), 1)
    return (1 - 2 * (parity % 2)).astype(f32) / jnp.sqrt(f32(order_size))


def dot(a, b, ca=1, cb=0):
    return lax.dot_general(a, b, (((ca,), (cb,)), ((), ())), preferred_element_type=f32)


def stack(value):
    return jnp.concatenate(
        [value[:, j * HB:(j + 1) * HB] for j in range(value.shape[1] // HB)], axis=0
    )


def unstack(value, rows):
    return jnp.concatenate(
        [value[j * rows:(j + 1) * rows] for j in range(value.shape[0] // rows)], axis=1
    )


def span(index, size):
    return pl.ds(pl.multiple_of(index * size, size), size)


def relay_kernel(
    sections, peers, x_in, top, weight_in, gain_in, signs, matrix, fb_in, flag,
    gout, dw, gain_out, fb,
    x, weight, gain, inbox, outbox, hidden, stage, pre, grad_act, right, sinv, gacc,
    gsum, gparts, own_part, sib_out, sib_in, chain_in,
    recv_sem, send_sem, out_sem, fb_sem, top_sem, own_sem, x_sem,
    w_recv, w_send, g_recv, g_send, s_recv, s_send, b_recv, b_send, c_recv, c_send,
):
    sec = lax.axis_index("section")
    here = lax.axis_index("fsdp")
    chips = peers // 2
    chip = here // 2
    core = lax.rem(here, 2)
    sibling = here + 1 - 2 * core
    rows_all, width = x.shape
    rank = weight.shape[1]
    shard = width // peers
    held = fb.shape[0]
    chunks = rows_all // CHUNK
    last = sections - 1
    wide = 1024
    barrier = pltpu.get_barrier_semaphore()

    for k in range(1, peers):
        pl.semaphore_signal(
            barrier, inc=1, device_id={"fsdp": lax.rem(here + k, peers)}, device_id_type=MESH
        )

    @pl.when(sec < last)
    def _():
        pl.semaphore_signal(barrier, inc=1, device_id={"section": sec + 1}, device_id_type=MESH)

    own_copy = pltpu.make_async_copy(weight_in, weight.at[span(here, shard)], own_sem)
    own_copy.start()
    x_copy = pltpu.make_async_copy(x_in, x, x_sem)
    x_copy.start()
    fb_copy = pltpu.make_async_copy(fb_in, fb, fb_sem)
    fb_copy.start()
    group_wide = GROUP * HB
    groups = width // group_wide
    top_copies = [
        pltpu.make_async_copy(
            top.at[:, pl.ds(k * group_wide, group_wide)],
            inbox.at[k, :, pl.ds(0, group_wide)],
            top_sem.at[k],
        )
        for k in range(groups)
    ]

    @pl.when(sec == last)
    def _():
        for copy in top_copies:
            copy.start()

    gain[:, span(here, shard)] = gain_in[...]
    gacc[...] = jnp.zeros_like(gacc)
    pre[...] = jnp.zeros_like(pre)
    grad_act[...] = jnp.zeros_like(grad_act)
    pl.semaphore_wait(barrier, peers - 1 + (sec > 0).astype(jnp.int32))

    own_copy.wait()

    def weight_copy(owner, target, way):
        return pltpu.make_async_remote_copy(
            src_ref=weight.at[span(owner, shard)],
            dst_ref=weight.at[span(owner, shard)],
            send_sem=w_send.at[way * chips + owner // 2],
            recv_sem=w_recv.at[owner],
            device_id={"fsdp": target},
            device_id_type=MESH,
        )

    def pass_right(owner, act):
        @pl.when(chip < chips - 1)
        def _():
            act(weight_copy(owner, here + 2, 0))

    def pass_left(owner, act):
        @pl.when(chip > 0)
        def _():
            act(weight_copy(owner, here - 2, 1))

    def pass_sibling(owner, act):
        act(weight_copy(owner, sibling, 2))

    def start(copy):
        copy.start()

    def finish(copy):
        copy.wait_send()

    def gain_copy(k):
        return pltpu.make_async_remote_copy(
            src_ref=gain.at[:, span(here, shard)],
            dst_ref=gain.at[:, span(here, shard)],
            send_sem=g_send.at[k],
            recv_sem=g_recv.at[k],
            device_id={"fsdp": lax.rem(here + k, peers)},
            device_id_type=MESH,
        )

    for k in range(1, peers):
        gain_copy(k).start()
    pass_right(here, start)
    pass_left(here, start)
    pass_sibling(here, start)

    swapped = jnp.broadcast_to(flag[0:1, 0:1], (CHUNK, wide)) == 1

    def exchange(ref, c, cols):
        here_rows, there_rows = span(c, CHUNK), span(c + chunks // 2, CHUNK)
        first = ref[here_rows, cols].astype(f32)
        second = ref[there_rows, cols].astype(f32)
        ref[here_rows, cols] = jnp.where(swapped, second, first).astype(bf16)
        ref[there_rows, cols] = jnp.where(swapped, first, second).astype(bf16)

    x_copy.wait()

    @pl.loop(0, chunks // 2)
    def _(c):
        @pl.loop(0, width // wide)
        def _(k):
            exchange(x, c, span(k, wide))

    @pl.loop(0, chunks)
    def _(c):
        rows = span(c, CHUNK)

        def square(k, acc):
            part = x[rows, span(k, wide)].astype(f32)
            part = part * part
            for j in range(wide // LANES):
                acc = acc + part[:, j * LANES:(j + 1) * LANES]
            return acc

        acc = lax.fori_loop(0, width // wide, square, jnp.zeros((CHUNK, LANES), f32))
        scale_inv = lax.rsqrt(jnp.sum(acc, axis=-1, keepdims=True) / width + eps_norm)
        sinv[rows, :] = jnp.broadcast_to(scale_inv, (CHUNK, LANES))

    for k in range(1, peers):
        pltpu.make_async_remote_copy(
            src_ref=gain.at[:, span(here, shard)],
            dst_ref=gain.at[:, span(lax.rem(here + peers - k, peers), shard)],
            send_sem=g_send.at[k],
            recv_sem=g_recv.at[k],
            device_id={"fsdp": lax.rem(here + k, peers)},
            device_id_type=MESH,
        ).wait_recv()

    @pl.loop(0, chunks)
    def _(c):
        rows = span(c, CHUNK)
        scale_inv = sinv[rows, 0:1]

        @pl.loop(0, width // wide)
        def _(k):
            cols = span(k, wide)
            hidden[rows, cols] = (x[rows, cols].astype(f32) * scale_inv * gain[:, cols]).astype(bf16)

    @pl.when(sec == last)
    def _():
        for copy in top_copies:
            copy.wait()

        @pl.loop(0, chunks // 2)
        def _(c):
            @pl.loop(0, groups)
            def _(k):
                for j in range(group_wide // wide):
                    exchange(inbox.at[k], c, pl.ds(j * wide, wide))

    def accumulate(spot):
        other = spot * 2 + 1 - core
        weight_copy(other, sibling, 2).wait_recv()
        for owner in (spot * 2 + core, other):
            cols = span(owner, shard)
            pre[...] += dot(hidden[:, cols], weight[cols, :])

            @pl.when(sec == last)
            def _():
                first = owner * shard
                part = pl.ds(pl.multiple_of(lax.rem(first, group_wide), shard), shard)
                grad_act[...] += dot(inbox[first // group_wide, :, part], weight[cols, :])

    def accumulate_around(distance):
        @pl.when(chip >= distance)
        def _():
            accumulate(chip - distance)

        if distance > 0:
            @pl.when(chip + distance < chips)
            def _():
                accumulate(chip + distance)

    for distance in range(1, chips):
        @pl.when(chip >= distance)
        def _():
            owner = here - 2 * distance
            weight_copy(owner, sibling, 2).wait_recv()
            pass_right(owner, start)
            pass_sibling(owner, start)

        @pl.when(chip + distance < chips)
        def _():
            owner = here + 2 * distance
            weight_copy(owner, sibling, 2).wait_recv()
            pass_left(owner, start)
            pass_sibling(owner, start)

        accumulate_around(distance - 1)
    accumulate_around(chips - 1)

    fb_copy.wait()
    lane = lax.broadcasted_iota(jnp.int32, (CHUNK, LANES), 1)

    def send(c, slot, k):
        return pltpu.make_async_remote_copy(
            src_ref=outbox.at[slot, k],
            dst_ref=inbox.at[k, span(c, CHUNK)],
            send_sem=send_sem.at[slot, k],
            recv_sem=recv_sem.at[c, k],
            device_id={"section": sec - 1},
            device_id_type=MESH,
        )

    def store(c, half):
        return pltpu.make_async_copy(stage.at[half], gout.at[span(c, CHUNK)], out_sem.at[half])

    @pl.loop(0, chunks)
    def _(c):
        rows = span(c, CHUNK)
        kept = span(lax.rem(c, held // CHUNK), CHUNK)
        half = lax.rem(c, 2)
        slot = lax.rem(c, SLOTS)

        @pl.when(c >= 2)
        def _():
            store(c - 2, half).wait()

        @pl.when(sec == last)
        def _():
            @pl.loop(0, groups)
            def _(k):
                stage[half, :, span(k, group_wide)] = inbox[k, rows, pl.ds(0, group_wide)].astype(f32)

        @pl.when(sec < last)
        def _():
            acc = jnp.zeros((CHUNK, rank), f32)
            held_low = None
            for k in range(groups):
                cols = pl.ds(k * group_wide, group_wide)
                send(c, slot, k).wait_recv()
                scales = inbox[k, rows, pl.ds(group_wide, LANES)].astype(f32)
                scale = jnp.concatenate([scales[:, j:j + 1] for j in range(GROUP)], axis=0)
                value = dot(stack(inbox[k, rows, pl.ds(0, group_wide)]), matrix[...]) * scale
                if k > 0:
                    acc = acc + dot(held_low, weight[pl.ds((k - 1) * group_wide, group_wide), :])
                value = unstack(value, CHUNK) * signs[1:2, cols]
                held_low = value.astype(bf16)
                stage[half, :, cols] = value
                inbox[k, rows, pl.ds(0, group_wide)] = held_low
            acc = acc + dot(held_low, weight[pl.ds((groups - 1) * group_wide, group_wide), :])
            grad_act[rows, :] = acc

        pre_here = pre[rows, :]
        sigma = jax.nn.sigmoid(pre_here)
        grad_pre = (grad_act[rows, :] * sigma * (1.0 + pre_here * (1.0 - sigma))).astype(bf16)
        right[rows, :] = grad_pre
        right[span(c + chunks, CHUNK), :] = (pre_here * sigma).astype(bf16)
        inner = jnp.sum(grad_pre.astype(f32) * pre_here, axis=-1, keepdims=True) / width
        scale_inv = sinv[rows, 0:1]

        def back(k):
            return dot(grad_pre, weight[pl.ds(k * group_wide, group_wide), :], 1, 1)

        def layer_block(cols, grad_hidden):
            normed = x[rows, cols].astype(f32) * scale_inv
            term = grad_hidden * normed
            total = term[0:8]
            for j in range(1, CHUNK // 8):
                total = total + term[8 * j:8 * j + 8]
            grad_out = stage[half, :, cols] + scale_inv * (grad_hidden * gain[:, cols] - normed * inner)
            return total, grad_out

        @pl.when(sec == 0)
        def _():
            for k in range(groups):
                cols = pl.ds(k * group_wide, group_wide)
                total, grad_out = layer_block(cols, back(k))
                gacc[:, cols] += total
                stage[half, :, cols] = grad_out

        @pl.when(sec > 0)
        def _():
            @pl.when(c >= SLOTS)
            def _():
                for k in range(groups):
                    send(c - SLOTS, slot, k).wait_send()

            following = back(0)
            for k in range(groups):
                cols = pl.ds(k * group_wide, group_wide)
                total, grad_out = layer_block(cols, following)
                if k + 1 < groups:
                    following = back(k + 1)
                value = grad_out + fb[kept, cols]
                sign = signs[0:1, cols]
                turned = stack(value * sign)
                high = turned.astype(bf16)
                low = (turned - high.astype(f32)).astype(bf16)
                rotated = dot(jnp.concatenate([high, low], axis=0), matrix[...])
                rotated = rotated[:GROUP * CHUNK] + rotated[GROUP * CHUNK:]
                scale = jnp.sum(jnp.abs(rotated), axis=-1, keepdims=True) / HB + eps_scale
                scale = scale.astype(bf16).astype(f32)
                levels = jnp.clip(rotated * (1.0 / scale), -1.0, 1.0).astype(bf16)
                decoded = unstack(dot(levels, matrix[...]) * scale, CHUNK) * sign
                gacc[:, cols] += total
                stage[half, :, cols] = grad_out
                outbox[slot, k, :, pl.ds(0, group_wide)] = unstack(levels, CHUNK)
                scales = jnp.zeros((CHUNK, LANES), f32)
                for j in range(GROUP):
                    scales = jnp.where(lane == j, scale[j * CHUNK:(j + 1) * CHUNK], scales)
                outbox[slot, k, :, pl.ds(group_wide, LANES)] = scales.astype(bf16)
                send(c, slot, k).start()
                fb[kept, cols] = value - decoded

        store(c, half).start()

    gsum[...] = jnp.sum(gacc[...], axis=0, keepdims=True)

    def sum_copy(k):
        target = lax.rem(here + k, peers)
        return pltpu.make_async_remote_copy(
            src_ref=gsum.at[:, span(target, shard)],
            dst_ref=gparts.at[k],
            send_sem=s_send.at[k],
            recv_sem=s_recv.at[k],
            device_id={"fsdp": target},
            device_id_type=MESH,
        )

    for k in range(1, peers):
        sum_copy(k).start()

    piece = 256

    def share(owner, into, spot):
        @pl.loop(0, shard // piece)
        def _(k):
            cols = pl.ds(pl.multiple_of(owner * shard + k * piece, piece), piece)
            first = owner * shard + k * piece
            part = pl.ds(pl.multiple_of(lax.rem(first, group_wide), piece), piece)
            left = jnp.concatenate([hidden[:, cols], inbox[first // group_wide, :, part]], axis=0)
            into[spot, span(k, piece), :] = dot(left, right[...], 0, 0).astype(bf16)

    def sibling_copy(spot):
        return pltpu.make_async_remote_copy(
            src_ref=sib_out.at[spot],
            dst_ref=sib_in.at[spot],
            send_sem=b_send.at[spot],
            recv_sem=b_recv.at[spot],
            device_id={"fsdp": sibling},
            device_id_type=MESH,
        )

    def chain_copy(spot, way):
        arrive = spot
        target = here + 2
        if way == 1:
            target = here - 2
            arrive = spot + (chips - spot) * (chip - 1 == spot).astype(jnp.int32)
        return pltpu.make_async_remote_copy(
            src_ref=own_part.at[spot],
            dst_ref=chain_in.at[arrive],
            send_sem=c_send.at[spot],
            recv_sem=c_recv.at[arrive],
            device_id={"fsdp": target},
            device_id_type=MESH,
        )

    def arrived(slot):
        pltpu.make_async_remote_copy(
            src_ref=own_part.at[0],
            dst_ref=chain_in.at[slot],
            send_sem=c_send.at[0],
            recv_sem=c_recv.at[slot],
            device_id={"fsdp": sibling},
            device_id_type=MESH,
        ).wait_recv()

    def merge(spot, inner_chip):
        sibling_copy(spot).wait_recv()

        @pl.when(inner_chip)
        def _():
            arrived(spot)

            @pl.loop(0, shard // piece)
            def _(k):
                part = span(k, piece)
                own_part[spot, part, :] = (
                    own_part[spot, part, :].astype(f32) + sib_in[spot, part, :].astype(f32)
                    + chain_in[spot, part, :].astype(f32)
                ).astype(bf16)

        @pl.when(jnp.logical_not(inner_chip))
        def _():
            @pl.loop(0, shard // piece)
            def _(k):
                part = span(k, piece)
                own_part[spot, part, :] = (
                    own_part[spot, part, :].astype(f32) + sib_in[spot, part, :].astype(f32)
                ).astype(bf16)

    def go_right(k):
        spot = chips - 1 - k

        @pl.when(spot > chip)
        def _():
            merge(spot, chip > 0)
            chain_copy(spot, 0).start()

    def go_left(k):
        @pl.when(k < chip)
        def _():
            merge(k, chip < chips - 1)
            chain_copy(k, 1).start()

    @pl.loop(0, chips)
    def _(k):
        low_half = (chip < chips // 2).astype(jnp.int32)
        spot = low_half * (chips - 1 - k) + (1 - low_half) * k
        share(spot * 2 + 1 - core, sib_out, spot)
        sibling_copy(spot).start()
        share(spot * 2 + core, own_part, spot)

        @pl.when(jnp.logical_and(chip == 0, k > 0))
        def _():
            go_right(k - 1)

        @pl.when(jnp.logical_and(chip == chips - 1, k > 0))
        def _():
            go_left(k - 1)

    @pl.loop(0, chips)
    def _(k):
        @pl.when(jnp.logical_and(chip > 0, chip < chips // 2))
        def _():
            go_right(k)
            go_left(k)

        @pl.when(jnp.logical_and(chip >= chips // 2, chip < chips - 1))
        def _():
            go_left(k)
            go_right(k)

    sibling_copy(chip).wait_recv()

    @pl.loop(0, shard // piece)
    def _(k):
        part = span(k, piece)
        dw[part, :] = own_part[chip, part, :].astype(f32) + sib_in[chip, part, :].astype(f32)

    def add_arrived(slot):
        arrived(slot)

        @pl.loop(0, shard // piece)
        def _(k):
            part = span(k, piece)
            dw[part, :] += chain_in[slot, part, :].astype(f32)

    @pl.when(chip > 0)
    def _():
        add_arrived(chip)

    @pl.when(chip < chips - 1)
    def _():
        add_arrived(chips)

    total = gsum[:, span(here, shard)]
    for k in range(1, peers):
        sum_copy(k).wait_recv()
        total = total + gparts[k]
    gain_out[...] = total

    for c in range(max(0, chunks - 2), chunks):
        store(c, c % 2).wait()

    @pl.when(sec > 0)
    def _():
        for c in range(max(0, chunks - SLOTS), chunks):
            for k in range(groups):
                send(c, c % SLOTS, k).wait_send()

    for k in range(1, peers):
        gain_copy(k).wait_send()
        sum_copy(k).wait_send()
    pass_right(here, finish)
    pass_left(here, finish)
    pass_sibling(here, finish)
    for distance in range(1, chips):
        @pl.when(chip >= distance)
        def _():
            pass_right(here - 2 * distance, finish)
            pass_sibling(here - 2 * distance, finish)

        @pl.when(chip + distance < chips)
        def _():
            pass_left(here + 2 * distance, finish)
            pass_sibling(here + 2 * distance, finish)

    @pl.loop(0, chips)
    def _(k):
        sibling_copy(k).wait_send()

        @pl.when(k > chip)
        def _():
            chain_copy(k, 0).wait_send()

        @pl.when(k < chip)
        def _():
            chain_copy(k, 1).wait_send()


def reorder_kernel(order, source, target):
    target[...] = source[...]


def reorder(order, array):
    micro_count, token_count, width = array.shape
    rows = 64
    return pl.pallas_call(
        reorder_kernel,
        out_shape=jax.ShapeDtypeStruct(array.shape, array.dtype),
        grid_spec=pltpu.PrefetchScalarGridSpec(
            num_scalar_prefetch=1,
            grid=(micro_count, token_count // rows),
            in_specs=[pl.BlockSpec((1, rows, width), lambda m, i, order: (m, i, 0))],
            out_specs=pl.BlockSpec((1, rows, width), lambda m, i, order: (order[m], i, 0)),
        ),
    )(order, array)


def per_device(
    section_inputs, top_grads, weights, norm_gains, feedback, rotation_bits, batch_order
):
    section_count = lax.axis_size("section")
    peers = lax.axis_size("fsdp")
    section_here = lax.axis_index("section")
    micro_count, token_count, width = section_inputs.shape[1:]
    shard, rank = weights.shape[1:]
    rows = micro_count * token_count
    chunks = rows // CHUNK
    chips = peers // 2
    groups = width // (GROUP * HB)
    above = jnp.minimum(section_here + 1, section_count - 1)
    bits = jnp.stack([rotation_bits[section_here], rotation_bits[above]])
    signs = (1 - 2 * bits).astype(f32)
    assert micro_count == 2
    flag = jnp.broadcast_to(batch_order[0], (1, LANES))
    vmem = pl.BlockSpec(memory_space=pltpu.VMEM)
    hbm = pl.BlockSpec(memory_space=pl.ANY)
    dma = pltpu.SemaphoreType.DMA
    gout, dw, gain_share, fb_out = pl.pallas_call(
        functools.partial(relay_kernel, section_count, peers),
        out_shape=(
            jax.ShapeDtypeStruct((rows, width), f32),
            jax.ShapeDtypeStruct((shard, rank), f32),
            jax.ShapeDtypeStruct((1, shard), f32),
            jax.ShapeDtypeStruct((token_count, width), f32),
        ),
        in_specs=[hbm, hbm, hbm, vmem, vmem, vmem, hbm, vmem],
        out_specs=(hbm, vmem, vmem, vmem),
        scratch_shapes=[
            pltpu.VMEM((rows, width), bf16),
            pltpu.VMEM((width, rank), bf16),
            pltpu.VMEM((1, width), f32),
            pltpu.VMEM((groups, rows, GROUP * HB + LANES), bf16),
            pltpu.VMEM((SLOTS, groups, CHUNK, GROUP * HB + LANES), bf16),
            pltpu.VMEM((rows, width), bf16),
            pltpu.VMEM((2, CHUNK, width), f32),
            pltpu.VMEM((rows, rank), f32),
            pltpu.VMEM((rows, rank), f32),
            pltpu.VMEM((2 * rows, rank), bf16),
            pltpu.VMEM((rows, LANES), f32),
            pltpu.VMEM((8, width), f32),
            pltpu.VMEM((1, width), f32),
            pltpu.VMEM((peers, 1, shard), f32),
            pltpu.VMEM((chips, shard, rank), bf16),
            pltpu.VMEM((chips, shard, rank), bf16),
            pltpu.VMEM((chips, shard, rank), bf16),
            pltpu.VMEM((chips + 1, shard, rank), bf16),
            dma((chunks, groups)), dma((SLOTS, groups)), dma((2,)), dma, dma((groups,)), dma, dma,
            dma((peers,)), dma((3 * chips,)),
            dma((peers,)), dma((peers,)),
            dma((peers,)), dma((peers,)),
            dma((chips,)), dma((chips,)),
            dma((chips + 1,)), dma((chips,)),
        ],
        compiler_params=pltpu.CompilerParams(
            collective_id=0, has_side_effects=True, vmem_limit_bytes=60 * 1024 * 1024
        ),
    )(
        section_inputs.reshape(rows, width), top_grads.reshape(rows, width), weights[0],
        norm_gains, signs, hadamard(HB).astype(bf16), feedback[0], flag,
    )
    input_grads = reorder(batch_order, gout.reshape(micro_count, token_count, width))
    return (input_grads[None], dw[None], gain_share, fb_out[None])


def solution(mesh):
    return jax.shard_map(
        per_device,
        mesh=mesh,
        in_specs=(
            P("section", None, "fsdp", None),
            P(None, "fsdp", None),
            P("section", "fsdp", None),
            P("section", "fsdp"),
            P("section", "fsdp", None),
            P(),
            P(),
        ),
        out_specs=(
            P("section", None, "fsdp", None),
            P("section", "fsdp", None),
            P("section", "fsdp"),
            P("section", "fsdp", None),
        ),
        check_vma=False,
    )
```
